32 devices in a mesh: dp: 4 (over z), fsdp: 2 (over x), tensor: 4 (over y, core).
Axes of the slice: x: 2, y: 2, z: 4, core: 2. Of those that a mesh axis runs over, the one named last changes fastest.
Arguments:
- candidates: bfloat16 [4, 16, 64, 4096], P('dp', 'fsdp', None, 'tensor'), may hold values from -40 to 40
- cand_lengths: int32 [4, 16], P('dp', 'fsdp'), may hold values from 1 to 64, 768 in all within a row
- pairing: int32 [4, 8, 2], P('dp'), may hold values from 0 to 15, as said below
- attn_gain: float32 [4096], replicated, may hold values from 0.1 to 1.9
- w_query: bfloat16 [4096, 4096], P('fsdp', 'tensor'), may hold values from -2 to 2
- w_key: bfloat16 [4096, 512], P('fsdp', 'tensor'), may hold values from -1 to 1
- w_value: bfloat16 [4096, 512], P('fsdp', 'tensor'), may hold values from -0.09375 to 0.09375
- w_out: bfloat16 [4096, 4096], P('tensor', 'fsdp'), may hold values from -0.09375 to 0.09375
- ffn_gain: float32 [4096], replicated, may hold values from 0.1 to 1.9
Outputs:
- resid: bfloat16 [4, 8, 128, 4096], P('dp', 'fsdp', None, 'tensor')
- normed: bfloat16 [4, 8, 128, 4096], P('dp', 'fsdp')
The draws below stay inside these ranges and needn't reach their ends.
Inputs may be any that keep to these rules, and one draw needn't show every extreme that they name: pairing[p] names each of the 16 candidates of prompt p exactly once. Candidates come in blocks of 8 consecutive indices and pair rows in blocks of 4; each block of candidates sends exactly 4 of its candidates to each of 2 blocks of pair rows.
All inputs are finite; a program needn't handle non-finite values. No bound on the sum of `cand_lengths` on one device may be relied on, other than what follows from the above.
Results may differ from the reference program's by a relative error of at most 0.018.
Values may be sent and summed in bfloat16 or wider, within the bound.
A program may use at most 192 MiB of HBM per device.

```python
import math
from functools import partial
import jax
import jax.numpy as jnp
import numpy as np
from jax import lax

D = 4096
QHEADS = 32
KVHEADS = 4
HEAD = 128
SAMPLE = 64
CAND_DEV = 8
CANDS = 16
PAIRS = 8
PROMPTS = 4
N_TENSOR = 4


def shared_base(key):
    return jnp.clip(jax.random.normal(key, (D, KVHEADS * HEAD), dtype=jnp.float32), -5.0, 5.0)


def draw_candidates(key, part):
    key = jax.random.fold_in(key, 21)
    keys = jax.random.split(key, 3)
    shape = (PROMPTS, CANDS, SAMPLE, D)
    row_scale = jnp.exp(jax.random.uniform(keys[1], (PROMPTS, CANDS, SAMPLE, 1), minval=-1.15, maxval=1.15))
    col_scale = jnp.exp(jax.random.uniform(keys[2], (D,), minval=-1.15, maxval=1.15))
    base = jnp.clip(jax.random.normal(keys[0], shape), -4.0, 4.0)
    values = jnp.clip(base * row_scale * col_scale, -40.0, 40.0)
    return values.astype(jnp.bfloat16)


def draw_w_key(key, part):
    base = shared_base(key)
    key = jax.random.fold_in(key, 31)
    extra = jnp.clip(jax.random.normal(key, (D, KVHEADS * HEAD)), -5.0, 5.0)
    values = (0.8 * base + 0.6 * extra) * D ** (-0.5)
    return jnp.clip(values, -1.0, 1.0).astype(jnp.bfloat16)


def draw_w_query(key, part):
    key = jax.random.fold_in(key, 32)
    keys = jax.random.split(key, 1)
    own = jnp.clip(jax.random.normal(keys[0], (D, QHEADS * HEAD)), -5.0, 5.0)
    values = own
    return jnp.clip(values * D ** (-0.5), -2.0, 2.0).astype(jnp.bfloat16)


def draw_pairing(key, part):
    key = jax.random.fold_in(key, 41)
    devices = CANDS // CAND_DEV
    reach = min(CAND_DEV, devices)

    def one_prompt(prompt_key):
        keys = jax.random.split(prompt_key, 3)
        offsets = jax.random.permutation(keys[0], devices)[:reach]
        order_keys = jax.random.split(keys[1], devices)
        local_order = jax.vmap(partial(jax.random.permutation, x=CAND_DEV))(order_keys)
        source = jnp.arange(devices, dtype=jnp.int32)[:, None]
        target = (source + offsets[local_order % reach]) % devices
        mixing = jax.random.permutation(keys[2], CANDS)
        scores = target.reshape(-1) * CANDS + mixing
        ordered = jnp.argsort(scores, stable=True)
        return ordered.astype(jnp.int32).reshape(PAIRS, 2)
    return jax.vmap(one_prompt)(jax.random.split(key, PROMPTS))


def level_of(key, dims, cuts, smallest, largest):
    def one(axis_at, blocks):
        draws = jax.random.uniform(jax.random.fold_in(jax.random.fold_in(key, 6), axis_at), (blocks,), jnp.float32, smallest / len(cuts), largest / len(cuts))
        return jnp.repeat(jnp.exp(draws), dims[axis_at] // blocks).reshape((-1,) + (1,) * (len(dims) - axis_at - 1))

    factor_of = one(*cuts[0])
    for cut in cuts[1:]:
        factor_of = factor_of * one(*cut)
    return factor_of


def length_profile(count, total, most, slope):
    weights = [(1 << 20) // math.isqrt(grade ** slope) + 1 for grade in range(2, count + 1)]
    rest, given = total - most - (count - 1), [1] * (count - 1)
    while rest > 0:
        free = [i for i in range(count - 1) if given[i] < most]
        whole, left = sum([weights[i] for i in free]), rest
        for i in free:
            addition = min(most - given[i], max(1, left * weights[i] // whole), rest)
            given[i] = given[i] + addition
            rest = rest - addition
    return np.array([most] + given)


def ragged_sizes(rng, number_of, total, bound, skew):
    if number_of == 2:
        one = jax.random.randint(rng, (), max(1, total - bound), min(bound, total - 1) + 1)
        return jnp.stack([one, total - one])
    sizes = jnp.asarray(length_profile(number_of, total, bound, skew), jnp.int32)
    pairs = (number_of - 1) // 2
    source_of, taker = sizes[1:1 + 2 * pairs:2], sizes[2:2 + 2 * pairs:2]
    margin = jnp.minimum(source_of - 1, bound - taker)
    shifted = jax.random.randint(jax.random.fold_in(rng, 1), (pairs,), 0, 1 << 20) % (margin + 1)
    sizes = sizes.at[1:1 + 2 * pairs:2].set(source_of - shifted).at[2:2 + 2 * pairs:2].set(taker + shifted)
    return sizes[jax.random.permutation(jax.random.fold_in(rng, 2), number_of)]


def bell_draw(rng, shape, scale, bound, cuts=(), kind=jnp.bfloat16):
    result = jax.random.normal(rng, shape, jnp.float32) * scale
    if len(cuts) > 0:
        result = level_of(rng, shape, cuts, -0.22, 0.18) * result
    return jnp.clip(result, min=-bound, max=bound).astype(kind)


def setup_inputs(seed: int = 0) -> dict:
    key_of = jax.random.split(jax.random.key(seed), 10)
    candidates = draw_candidates(jax.random.fold_in(key_of[9], 71), 0)
    cand_lengths = jax.vmap(lambda own: ragged_sizes(own, CANDS, CANDS * SAMPLE * 3 // 4, SAMPLE, 1))(jax.random.split(key_of[1], PROMPTS)).reshape((PROMPTS, CANDS)).astype(jnp.int32)
    pairing = draw_pairing(jax.random.fold_in(key_of[9], 71), 0)
    attn_gain = jnp.clip(1.0 + 0.18 * jax.random.normal(key_of[3], (D,), jnp.float32), 0.1, 1.9)
    w_query = draw_w_query(jax.random.fold_in(key_of[9], 71), 0)
    w_key = draw_w_key(jax.random.fold_in(key_of[9], 71), 0)
    w_value = bell_draw(key_of[6], (D, KVHEADS * HEAD), D ** -0.5, 0.09375, ((0, 2), (1, 4)))
    w_out = bell_draw(key_of[7], (QHEADS * HEAD, D), (QHEADS * HEAD) ** -0.5, 0.09375, ((0, 4), (1, 2)))
    ffn_gain = jnp.clip(1.0 + 0.18 * jax.random.normal(key_of[8], (D,), jnp.float32), 0.1, 1.9)
    return {"candidates": candidates, "cand_lengths": cand_lengths, "pairing": pairing, "attn_gain": attn_gain, "w_query": w_query, "w_key": w_key, "w_value": w_value, "w_out": w_out, "ffn_gain": ffn_gain}


epsilon = 1e-05
rope_base = 500000.0

def rms_scale(values, gain):
    mean_square = lax.optimization_barrier(jnp.mean(values * values, axis=-1, keepdims=True))
    return values * lax.rsqrt(mean_square + epsilon) * gain

def positions_of(lengths, sample):
    slot_steps = jnp.arange(2 * sample, dtype=jnp.int32)
    return jnp.where(slot_steps < sample, slot_steps, lengths[..., :1] + slot_steps - sample)

def key_mask(lengths, sample):
    slot_steps = jnp.arange(2 * sample, dtype=jnp.int32)
    local_step = jnp.where(slot_steps < sample, slot_steps, slot_steps - sample)
    limit = jnp.where(slot_steps < sample, lengths[..., :1], lengths[..., 1:])
    valid = local_step < limit
    causal = slot_steps[None, :] <= slot_steps[:, None]
    return causal[None] & valid[:, None, :]

def rotate(values, positions, head_size):
    half = head_size // 2
    inv_freq = rope_base ** (-jnp.arange(half, dtype=jnp.float32) * 2.0 / head_size)
    angles = positions.astype(jnp.float32)[..., None] * inv_freq
    cosine = jnp.cos(angles)[..., None, :]
    sine_table = jnp.sin(angles)[..., None, :]
    lower = values[..., :half]
    upper = values[..., half:]
    return jnp.concatenate([lower * cosine - upper * sine_table, upper * cosine + lower * sine_table], axis=-1)

def attend(query, key_rows, value_rows, allowed):
    pair_rows, row_count, kv_count, group_size, head_size = query.shape
    scores = jnp.einsum('bqkgd,bskd->bkgqs', query.astype(jnp.float32), key_rows.astype(jnp.float32)) * head_size ** (-0.5)
    scores = jnp.where(allowed[:, None, None], scores, -1e+30)
    row_peak = lax.optimization_barrier(jnp.max(scores, axis=-1, keepdims=True))
    weights = jnp.exp(scores - row_peak)
    prob_rows = (weights / lax.optimization_barrier(jnp.sum(weights, axis=-1, keepdims=True))).astype(jnp.bfloat16)
    mixed_rows = jnp.einsum('bkgqs,bskd->bqkgd', prob_rows.astype(jnp.float32), value_rows.astype(jnp.float32))
    return mixed_rows.astype(jnp.bfloat16).reshape(pair_rows, row_count, kv_count * group_size * head_size)

def reference(candidates, cand_lengths, pairing, attn_gain, w_query, w_key, w_value, w_out, ffn_gain):

    def one_prompt(packed):
        cand_rows, lengths, pair_table = packed
        pair_count = pair_table.shape[0]
        sample = cand_rows.shape[1]
        width = cand_rows.shape[2]
        chosen = pair_table.reshape(-1).astype(jnp.int32)
        joined = jnp.take(cand_rows, chosen, axis=0).reshape(pair_count, 2 * sample, width)
        row_lengths = jnp.take(lengths, chosen, axis=0).reshape(pair_count, 2)
        inputs = joined.astype(jnp.float32).reshape(-1, width)
        normal_rows = rms_scale(inputs, attn_gain).astype(jnp.bfloat16)
        query = jnp.dot(normal_rows, w_query, preferred_element_type=jnp.float32)
        key_rows = jnp.dot(normal_rows, w_key, preferred_element_type=jnp.float32)
        value_rows = jnp.dot(normal_rows, w_value, preferred_element_type=jnp.float32)
        positions = positions_of(row_lengths, sample)
        query = rotate(query.reshape(pair_count, 2 * sample, QHEADS, HEAD), positions, HEAD).astype(jnp.bfloat16)
        key_rows = rotate(key_rows.reshape(pair_count, 2 * sample, KVHEADS, HEAD), positions, HEAD).astype(jnp.bfloat16)
        value_rows = value_rows.astype(jnp.bfloat16).reshape(pair_count, 2 * sample, KVHEADS, HEAD)
        query = query.reshape(pair_count, 2 * sample, KVHEADS, QHEADS // KVHEADS, HEAD)
        mixed = attend(query, key_rows, value_rows, key_mask(row_lengths, sample)).reshape(-1, QHEADS * HEAD)
        group_cols = QHEADS * HEAD // N_TENSOR
        branch = jnp.zeros((mixed.shape[0], width), jnp.float32)
        for group in range(N_TENSOR):
            term = jnp.dot(mixed[:, group * group_cols:(group + 1) * group_cols], w_out[group * group_cols:(group + 1) * group_cols], preferred_element_type=jnp.float32)
            rounded = lax.optimization_barrier(term.astype(jnp.bfloat16))
            branch = branch + rounded.astype(jnp.float32)
        stream = inputs + branch
        resid = stream.astype(jnp.bfloat16).reshape(pair_count, 2 * sample, width)
        normed = rms_scale(stream, ffn_gain).astype(jnp.bfloat16).reshape(pair_count, 2 * sample, width)
        return (resid, normed)
    resid, normed = lax.map(one_prompt, (candidates, cand_lengths, pairing))
    return (resid, normed)
```

```python
import jax
import jax.numpy as jnp
import numpy as np
from jax import lax
from jax.experimental import pallas as pl
from jax.experimental.pallas import tpu as pltpu
from jax.sharding import PartitionSpec as P

HEAD = 128


epsilon = 1e-05
rope_base = 500000.0


def rms_scale(values, gain):
    mean_square = jnp.mean(values * values, axis=-1, keepdims=True)
    return values * lax.rsqrt(mean_square + epsilon) * gain


def positions_of(lengths, sample):
    slot_steps = jnp.arange(2 * sample, dtype=jnp.int32)
    return jnp.where(slot_steps < sample, slot_steps, lengths[..., :1] + slot_steps - sample)


def key_mask(lengths, sample):
    slot_steps = jnp.arange(2 * sample, dtype=jnp.int32)
    local_step = jnp.where(slot_steps < sample, slot_steps, slot_steps - sample)
    limit = jnp.where(slot_steps < sample, lengths[..., :1], lengths[..., 1:])
    valid = local_step < limit
    causal = slot_steps[None, :] <= slot_steps[:, None]
    return causal[None] & valid[:, None, :]


def rotate(values, positions, head_size):
    half = head_size // 2
    inv_freq = rope_base ** (-jnp.arange(half, dtype=jnp.float32) * 2.0 / head_size)
    angles = positions.astype(jnp.float32)[..., None] * inv_freq
    cosine = jnp.cos(angles)[..., None, :]
    sine_table = jnp.sin(angles)[..., None, :]
    lower = values[..., :half]
    upper = values[..., half:]
    return jnp.concatenate(
        [lower * cosine - upper * sine_table, upper * cosine + lower * sine_table], axis=-1
    )


def attend(query, key_rows, value_rows, allowed):
    pair_rows, row_count, kv_count, group_size, head_size = query.shape
    scores = jnp.einsum(
        "bqkgd,bskd->bkgqs", query, key_rows, preferred_element_type=jnp.float32
    ) * head_size ** (-0.5)
    scores = jnp.where(allowed[:, None, None], scores, -1e30)
    row_peak = jnp.max(scores, axis=-1, keepdims=True)
    weights = jnp.exp(scores - row_peak)
    prob_rows = (weights / jnp.sum(weights, axis=-1, keepdims=True)).astype(jnp.bfloat16)
    mixed_rows = jnp.einsum(
        "bkgqs,bskd->bqkgd", prob_rows, value_rows, preferred_element_type=jnp.float32
    )
    return mixed_rows.astype(jnp.bfloat16).reshape(
        pair_rows * row_count, kv_count * group_size * head_size
    )


def on_device(
    candidates, cand_lengths, pairing, attn_gain, w_query, w_key, w_value, w_out, ffn_gain
):
    fsdp_count = lax.axis_size("fsdp")
    my_index = lax.axis_index("fsdp")
    cand_dev = candidates.shape[1]
    sample = candidates.shape[2]
    share_width = candidates.shape[3]
    pair_dev = cand_dev // 2
    most_slots = max(1, cand_dev // fsdp_count)
    flat_slots = pairing[0].reshape(-1)
    slot_count = flat_slots.shape[0]
    every_slot = jnp.arange(slot_count, dtype=jnp.int32)
    matches = flat_slots[:, None] == every_slot[None, :]
    target_slot = jnp.sum(jnp.where(matches, every_slot[:, None], 0), axis=0)
    target_dev = target_slot // cand_dev
    source_dev = every_slot // cand_dev
    earlier = (
        (source_dev[:, None] == source_dev[None, :])
        & (target_dev[:, None] == target_dev[None, :])
        & (every_slot[None, :] < every_slot[:, None])
    )
    send_rank = jnp.sum(earlier.astype(jnp.int32), axis=1)
    place = target_dev * most_slots + send_rank
    arrive = source_dev * most_slots + send_rank
    own_cands = my_index * cand_dev + jnp.arange(cand_dev, dtype=jnp.int32)
    own_pick = own_cands[:, None] == every_slot[None, :]
    own_place = jnp.sum(jnp.where(own_pick, place[None, :], 0), axis=1)
    buffer_slots = jnp.arange(fsdp_count * most_slots, dtype=jnp.int32)
    sender = buffer_slots[:, None] == own_place[None, :]
    outgoing = jnp.einsum(
        "bc,csf->bsf",
        sender.astype(jnp.bfloat16),
        candidates[0],
        preferred_element_type=jnp.float32,
    ).astype(jnp.bfloat16)
    out_lengths = jnp.sum(jnp.where(sender, cand_lengths[0][None, :], 0), axis=1)
    incoming, in_lengths = (
        lax.all_to_all(
            outgoing.reshape(fsdp_count, most_slots, sample, share_width),
            "fsdp",
            split_axis=0,
            concat_axis=0,
            tiled=True,
        ),
        lax.all_to_all(
            out_lengths.reshape(fsdp_count, most_slots),
            "fsdp",
            split_axis=0,
            concat_axis=0,
            tiled=True,
        ),
    )
    slot_pick = own_cands[:, None] == every_slot[None, :]
    wanted = jnp.sum(jnp.where(slot_pick, flat_slots[None, :], 0), axis=1)
    wanted_pick = wanted[:, None] == every_slot[None, :]
    wanted_from = jnp.sum(jnp.where(wanted_pick, arrive[None, :], 0), axis=1)
    receiver = wanted_from[:, None] == buffer_slots[None, :]
    local_rows = jnp.einsum(
        "cb,bsf->csf",
        receiver.astype(jnp.bfloat16),
        incoming.reshape(-1, sample, share_width),
        preferred_element_type=jnp.float32,
    ).astype(jnp.bfloat16)
    row_lengths = (
        jnp.sum(jnp.where(receiver, in_lengths.reshape(-1)[None, :], 0), axis=1)
        .astype(jnp.int32)
        .reshape(pair_dev, 2)
    )
    full_rows = lax.all_gather(local_rows, "tensor", axis=2, tiled=True)
    width = full_rows.shape[2]
    tok_count = cand_dev * sample
    inputs = full_rows.reshape(tok_count, width).astype(jnp.float32)
    normal_rows = rms_scale(inputs, attn_gain).astype(jnp.bfloat16)
    query_cols = w_query.shape[1]
    key_cols = w_key.shape[1]
    query = jnp.dot(
        normal_rows,
        lax.all_gather(w_query, "fsdp", axis=0, tiled=True),
        preferred_element_type=jnp.float32,
    )
    key_rows = jnp.dot(
        normal_rows,
        lax.all_gather(w_key, "fsdp", axis=0, tiled=True),
        preferred_element_type=jnp.float32,
    )
    value_rows = jnp.dot(
        normal_rows,
        lax.all_gather(w_value, "fsdp", axis=0, tiled=True),
        preferred_element_type=jnp.float32,
    )
    heads_here = query_cols // HEAD
    kv_here = key_cols // HEAD
    positions = positions_of(row_lengths, sample)
    query = rotate(query.reshape(pair_dev, 2 * sample, heads_here, HEAD), positions, HEAD).astype(
        jnp.bfloat16
    )
    key_rows = rotate(
        key_rows.reshape(pair_dev, 2 * sample, kv_here, HEAD), positions, HEAD
    ).astype(jnp.bfloat16)
    value_rows = value_rows.astype(jnp.bfloat16).reshape(pair_dev, 2 * sample, kv_here, HEAD)
    query = query.reshape(pair_dev, 2 * sample, kv_here, heads_here // kv_here, HEAD)
    mixed = attend(query, key_rows, value_rows, key_mask(row_lengths, sample))
    branch = jnp.dot(
        mixed, lax.all_gather(w_out, "fsdp", axis=1, tiled=True), preferred_element_type=jnp.float32
    )
    tensor_offset = lax.axis_index("tensor") * share_width
    summed_branch = lax.psum(branch.astype(jnp.bfloat16), "tensor").astype(jnp.float32)
    stream = inputs + summed_branch
    normed = rms_scale(stream, ffn_gain).astype(jnp.bfloat16)
    resid = lax.dynamic_slice_in_dim(stream, tensor_offset, share_width, 1).astype(jnp.bfloat16)
    return (
        resid.reshape(1, pair_dev, 2 * sample, share_width),
        normed.reshape(1, pair_dev, 2 * sample, width),
    )


MESH = pl.DeviceIdType.MESH
CH = 4
X1, Y1, S1A, S1B, XQ, XS, XM, SB, YB, XR, YR1, YR2, SR0, SR1, SR2, SR3, LN = range(17)


def plane_kernel(
    pair_ref, lens_ref, gain1_ref, gain2_ref, cos_ref, sin_ref, freq_ref,
    cand_ref, wq_ref, wk_ref, wv_ref, wo_ref,
    resid_ref, normed_ref,
    grid_x, relay, lhs, w_in, w_out, q_send, q_recv, q_own, ss_own, ss_recv, lens_all,
    mix_own, mix_recv, acc_own, sib_send, sib_recv, y_send, y_recv, x_send, stream, out_rows,
    send_sem, recv_sem, load_sem, local_sem, store_sem,
):
    f = lax.axis_index("fsdp")
    t = lax.axis_index("tensor")
    y = t // 2
    c = t % 2
    x_dev = {"fsdp": 1 - f}
    t_y = (t + 2) % 4
    t_s = t + 1 - 2 * c
    t_sy = (t_s + 2) % 4
    y_dev = {"tensor": t_y}
    s_dev = {"tensor": t_s}
    even = f == y

    def remote(kind, j, src, dst, dev):
        return pltpu.make_async_remote_copy(
            src_ref=src, dst_ref=dst, send_sem=send_sem.at[kind, j],
            recv_sem=recv_sem.at[kind, j], device_id=dev, device_id_type=MESH,
        )

    loads = []

    def load(src, dst):
        copy = pltpu.make_async_copy(src, dst, load_sem.at[len(loads)])
        copy.start()
        loads.append(copy)

    mine = pl.multiple_of(f * 512, 512)
    other = pl.multiple_of((1 - f) * 512, 512)
    load(wq_ref.at[:, pl.ds(mine, 512)], w_in.at[:, 0:512])
    load(wq_ref.at[:, pl.ds(other, 512)], w_in.at[:, 512:1024])
    load(wk_ref, w_in.at[:, 1024:1152])
    load(wv_ref, w_in.at[:, 1152:1280])
    for r, row in enumerate((mine, other)):
        for b, block in enumerate((t, t_y, t_s, t_sy)):
            load(
                wo_ref.at[pl.ds(row, 512), pl.ds(pl.multiple_of(block * 512, 512), 512)],
                w_out.at[r * 512:(r + 1) * 512, b * 512:(b + 1) * 512],
            )

    barrier = pltpu.get_barrier_semaphore()
    for dev in (x_dev, y_dev, s_dev):
        pl.semaphore_signal(barrier, inc=1, device_id=dev, device_id_type=MESH)
    pl.semaphore_wait(barrier, 3)

    lens_copy = remote(LN, 0, lens_ref, lens_all.at[pl.ds(pl.multiple_of(f * 8, 8), 8)], x_dev)
    lens_copy.start()
    lens_all[pl.ds(pl.multiple_of(f * 8, 8), 8), :] = lens_ref[...]

    cols = pl.ds(pl.multiple_of(c * 1024, 1024), 1024)

    def place(g, j):
        return grid_x.at[pl.ds(g * 8 + 2 * j, 2), :, cols]

    def own(j):
        return cand_ref.at[2 * j:2 * j + 2]

    def hop(j):
        return relay.at[2 * j:2 * j + 2]

    def local_copy(j):
        return pltpu.make_async_copy(own(j), place(f, j), local_sem.at[j])

    for j in range(CH):

        @pl.when(even)
        def _():
            remote(Y1, j, own(j), place(f, j), y_dev).start()
            local_copy(j).start()

        @pl.when(jnp.logical_not(even))
        def _():
            remote(Y1, j, own(j), hop(j), y_dev).start()
            remote(X1, j, own(j), place(f, j), x_dev).start()

    for copy in loads[:4]:
        copy.wait()

    def finish(j):
        remote(XQ, j, q_send.at[j], q_recv.at[j], x_dev).wait_recv()
        remote(XS, j, ss_own.at[j], ss_recv.at[j], x_dev).wait_recv()
        total = (ss_own[j] + ss_recv[j])[0:1, :]
        scale = lax.rsqrt(total * (1.0 / 4096.0) + epsilon)
        column = jnp.broadcast_to(scale, (128, 256)).T
        for m in range(6):
            part = slice(m * 128, (m + 1) * 128)
            summed = q_own[4 * j:4 * j + 4, :, part].reshape(256, 128) + q_recv[
                j, :, part
            ].astype(jnp.float32)
            q_own[4 * j:4 * j + 4, :, part] = (summed * column).reshape(4, 64, 128)

    for j in range(CH):

        @pl.when(even)
        def _():
            remote(Y1, j, own(j), hop(j), y_dev).wait_recv()
            remote(X1, j, hop(j), place(f, j), x_dev).start()
            local_copy(j).wait()

        @pl.when(jnp.logical_not(even))
        def _():
            remote(Y1, j, own(j), place(f, j), y_dev).wait_recv()

        remote(S1A, j, place(f, j), place(f, j), s_dev).start()
        remote(X1, j, own(j), place(1 - f, j), x_dev).wait_recv()
        remote(S1B, j, place(1 - f, j), place(1 - f, j), s_dev).start()
        remote(S1A, j, place(f, j), place(f, j), s_dev).wait_recv()
        remote(S1B, j, place(1 - f, j), place(1 - f, j), s_dev).wait_recv()

        gain = gain1_ref[f]
        for g in range(2):
            values = grid_x[g * 8 + 2 * j:g * 8 + 2 * j + 2].reshape(128, 2048).astype(jnp.float32)
            squares = jnp.sum(values * values, axis=1, keepdims=True)
            ss_own[j, :, g * 128:(g + 1) * 128] = jnp.broadcast_to(squares, (128, 128)).T[0:8]
            lhs[g * 128:(g + 1) * 128, :] = (values * gain).astype(jnp.bfloat16)

        def project(n):
            return jnp.dot(
                lhs[...],
                w_in[:, pl.ds(pl.multiple_of(n * 256, 256), 256)],
                preferred_element_type=jnp.float32,
            )

        @pl.loop(0, 3)
        def _(n):
            result = project(n + 2)
            at = pl.ds(pl.multiple_of(n * 256, 256), 256)
            q_send[j, :, at] = result.astype(jnp.bfloat16)

        q_own[4 * j:4 * j + 4, :, 512:768] = project(4).reshape(4, 64, 256)
        remote(XQ, j, q_send.at[j], q_recv.at[j], x_dev).start()
        remote(XS, j, ss_own.at[j], ss_recv.at[j], x_dev).start()

        @pl.loop(0, 2)
        def _(n):
            result = project(n)
            at = pl.ds(pl.multiple_of(n * 256, 256), 256)
            q_own[4 * j:4 * j + 4, :, at] = result.reshape(4, 64, 256)

        if j > 0:
            finish(j - 1)
    finish(CH - 1)
    lens_copy.wait()

    lane = lax.broadcasted_iota(jnp.int32, (1, 128), 1)
    sign = jnp.where(lane < 64, -1.0, 1.0)
    slot_t = lax.broadcasted_iota(jnp.int32, (128, 128), 0)
    slot_u = lax.broadcasted_iota(jnp.int32, (128, 128), 1)

    def packed(cand):
        return ((cand % 8) // 2) * 4 + (cand // 8) * 2 + cand % 2

    def attention(k, half):
        row = half * 4 + k
        cand0, cand1 = pair_ref[row, 0], pair_ref[row, 1]
        at0, at1 = packed(cand0), packed(cand1)
        len0 = lens_all[pl.ds(cand0, 1), :]
        len1 = lens_all[pl.ds(cand1, 1), :]
        angle = len0.astype(jnp.float32) * freq_ref[...]
        shift_cos, shift_sin = jnp.cos(angle), jnp.sin(angle)
        cos0, sin0 = cos_ref[...], sin_ref[...]
        cosine = jnp.concatenate([cos0, cos0 * shift_cos - sin0 * shift_sin], axis=0)
        sine = jnp.concatenate([sin0, sin0 * shift_cos + cos0 * shift_sin], axis=0) * sign
        allowed = (slot_u <= slot_t) & (lane < jnp.where(lane < 64, len0, len1 + 64))

        def block(m):
            part = slice(m * 128, (m + 1) * 128)
            return jnp.concatenate([q_own[at0, :, part], q_own[at1, :, part]], axis=0)

        def turned(m):
            values = block(m)
            return (values * cosine + pltpu.roll(values, 64, axis=1) * sine).astype(jnp.bfloat16)

        keys = turned(4)
        value_rows = block(5).astype(jnp.bfloat16)
        for h in range(4):
            scores = lax.dot_general(
                turned(h), keys, (((1,), (1,)), ((), ())), preferred_element_type=jnp.float32
            ) * HEAD ** (-0.5)
            scores = jnp.where(allowed, scores, -1e30)
            weights = jnp.exp(scores - jnp.max(scores, axis=1, keepdims=True))
            probs = weights / jnp.sum(weights, axis=1, keepdims=True)
            mixed = jnp.dot(
                probs.astype(jnp.bfloat16), value_rows, preferred_element_type=jnp.float32
            )
            mix_own[k, half * 128:(half + 1) * 128, h * 128:(h + 1) * 128] = mixed.astype(
                jnp.bfloat16
            )

    def stream_at(block, k):
        return stream.at[block, k]

    def own_block(k):
        return stream_at(f * 4 + t, k)

    def far_block(k):
        return stream_at((1 - f) * 4 + t, k)

    def share(kind, ref, k, dev):
        return remote(kind, k, ref, ref, dev)

    def mix_copy(k):
        return remote(XM, k, mix_own.at[k], mix_recv.at[k], x_dev)

    def partial_copy(k):
        return remote(SB, k, sib_send.at[k], sib_recv.at[k], s_dev)

    def pair_copy(k):
        return remote(YB, k, y_send.at[k], y_recv.at[k], y_dev)

    def cross_copy(k):
        return remote(XR, k, x_send.at[k], own_block(k), x_dev)

    def project_out(k):
        mix_copy(k).wait_recv()

        def term(n):
            at = pl.ds(pl.multiple_of(n * 256, 256), 256)
            return jnp.dot(
                mix_own[k], w_out[0:512, at], preferred_element_type=jnp.float32
            ) + jnp.dot(mix_recv[k], w_out[512:1024, at], preferred_element_type=jnp.float32)

        @pl.loop(0, 4)
        def _(n):
            at = pl.ds(pl.multiple_of(n * 256, 256), 256)
            sib_send[k, :, at] = term(n + 4).astype(jnp.bfloat16)

        partial_copy(k).start()

        @pl.loop(0, 4)
        def _(n):
            acc_own[k, :, pl.ds(pl.multiple_of(n * 256, 256), 256)] = term(n)

    def add_sibling(k):
        partial_copy(k).wait_recv()
        y_send[k] = (acc_own[k, :, 512:] + sib_recv[k, :, 512:].astype(jnp.float32)).astype(
            jnp.bfloat16
        )
        pair_copy(k).start()
        acc_own[k, :, 0:512] = acc_own[k, :, 0:512] + sib_recv[k, :, 0:512].astype(jnp.float32)

    def add_rows(k):
        pair_copy(k).wait_recv()
        at = pl.ds(pl.multiple_of(t * 512, 512), 512)
        parts = []
        for half in range(2):
            row = half * 4 + k
            rows = jnp.concatenate(
                [grid_x[pair_ref[row, 0], :, at], grid_x[pair_ref[row, 1], :, at]], axis=0
            )
            part = slice(half * 128, (half + 1) * 128)
            branch = acc_own[k, part, 0:512] + y_recv[k, part, :].astype(jnp.float32)
            parts.append(rows.astype(jnp.float32) + branch)
        first = f == 0
        x_send[k] = jnp.where(first, parts[1], parts[0]).astype(jnp.bfloat16)
        cross_copy(k).start()
        stream[f * 4 + t, k] = jnp.where(first, parts[0], parts[1]).astype(jnp.bfloat16)
        share(YR1, own_block(k), k, y_dev).start()
        share(SR0, own_block(k), k, s_dev).start()

    def pass_far(k):
        remote(XR, k, x_send.at[k], far_block(k), x_dev).wait_recv()
        share(YR2, far_block(k), k, y_dev).start()
        share(SR1, far_block(k), k, s_dev).start()

    def pass_pair(k):
        near = stream_at(f * 4 + t_y, k)
        far = stream_at((1 - f) * 4 + t_y, k)
        share(YR1, near, k, y_dev).wait_recv()
        share(SR2, near, k, s_dev).start()
        share(YR2, far, k, y_dev).wait_recv()
        share(SR3, far, k, s_dev).start()

    def resid_copy(k, b):
        return pltpu.make_async_copy(
            stream.at[2 * t + b, k],
            resid_ref.at[k, :, b * 512:(b + 1) * 512],
            store_sem.at[k, b],
        )

    def normed_copy(k):
        return pltpu.make_async_copy(out_rows.at[k], normed_ref.at[k], store_sem.at[k, 2])

    def norm(k):
        share(SR0, stream_at(f * 4 + t_s, k), k, s_dev).wait_recv()
        share(SR1, stream_at((1 - f) * 4 + t_s, k), k, s_dev).wait_recv()
        share(SR2, stream_at(f * 4 + t_sy, k), k, s_dev).wait_recv()
        share(SR3, stream_at((1 - f) * 4 + t_sy, k), k, s_dev).wait_recv()
        resid_copy(k, 0).start()
        resid_copy(k, 1).start()
        squares = jnp.zeros((128, 512), jnp.float32)
        for b in range(8):
            values = stream[b, k].astype(jnp.float32)
            squares = squares + values * values
        scale = lax.rsqrt(jnp.sum(squares, axis=1, keepdims=True) * (1.0 / 4096.0) + epsilon)
        for b in range(8):
            part = slice(b * 512, (b + 1) * 512)
            out_rows[k, :, part] = (
                stream[b, k].astype(jnp.float32) * scale * gain2_ref[:, part]
            ).astype(jnp.bfloat16)
        normed_copy(k).start()

    for copy in loads[4:]:
        copy.wait()
    stages = (project_out, add_sibling, add_rows, pass_far, pass_pair, norm)
    for step in range(CH + len(stages)):
        if step < CH:
            attention(step, 0)
            attention(step, 1)
            mix_copy(step).start()
        for late in range(len(stages) - 1, -1, -1):
            k = step - 1 - late
            if 0 <= k < CH:
                stages[late](k)

    for j in range(CH):

        @pl.when(even)
        def _():
            remote(Y1, j, own(j), place(f, j), y_dev).wait_send()
            remote(X1, j, hop(j), place(f, j), x_dev).wait_send()

        @pl.when(jnp.logical_not(even))
        def _():
            remote(Y1, j, own(j), hop(j), y_dev).wait_send()
            remote(X1, j, own(j), place(f, j), x_dev).wait_send()

        remote(S1A, j, place(f, j), place(f, j), s_dev).wait_send()
        remote(S1B, j, place(1 - f, j), place(1 - f, j), s_dev).wait_send()
        remote(XQ, j, q_send.at[j], q_recv.at[j], x_dev).wait_send()
        remote(XS, j, ss_own.at[j], ss_recv.at[j], x_dev).wait_send()
        mix_copy(j).wait_send()
        partial_copy(j).wait_send()
        pair_copy(j).wait_send()
        cross_copy(j).wait_send()
        share(YR1, own_block(j), j, y_dev).wait_send()
        share(SR0, own_block(j), j, s_dev).wait_send()
        share(YR2, far_block(j), j, y_dev).wait_send()
        share(SR1, far_block(j), j, s_dev).wait_send()
        share(SR2, stream_at(f * 4 + t_y, j), j, s_dev).wait_send()
        share(SR3, stream_at((1 - f) * 4 + t_y, j), j, s_dev).wait_send()
        resid_copy(j, 0).wait()
        resid_copy(j, 1).wait()
        normed_copy(j).wait()


def on_plane(
    candidates, cand_lengths, pairing, attn_gain, w_query, w_key, w_value, w_out, ffn_gain
):
    half = HEAD // 2
    inv_freq = np.float32(rope_base) ** (-np.arange(half, dtype=np.float32) * 2.0 / HEAD)
    freq = np.concatenate([inv_freq, inv_freq]).astype(np.float32)[None, :]
    angles = (np.arange(64, dtype=np.float32)[:, None] * freq).astype(np.float64)
    lens = jnp.broadcast_to(cand_lengths.reshape(8, 1), (8, 128))
    bf16, f32 = jnp.bfloat16, jnp.float32
    vmem = pl.BlockSpec(memory_space=pltpu.VMEM)
    hbm = pl.BlockSpec(memory_space=pl.ANY)
    resid, normed = pl.pallas_call(
        plane_kernel,
        out_shape=(
            jax.ShapeDtypeStruct((4, 128, 1024), bf16),
            jax.ShapeDtypeStruct((4, 128, 4096), bf16),
        ),
        in_specs=[pl.BlockSpec(memory_space=pltpu.SMEM)] + [vmem] * 6 + [hbm] * 5,
        out_specs=(hbm, hbm),
        scratch_shapes=[
            pltpu.VMEM((16, 64, 2048), bf16),
            pltpu.VMEM((8, 64, 1024), bf16),
            pltpu.VMEM((256, 2048), bf16),
            pltpu.VMEM((2048, 1280), bf16),
            pltpu.VMEM((1024, 2048), bf16),
            pltpu.VMEM((CH, 256, 768), bf16),
            pltpu.VMEM((CH, 256, 768), bf16),
            pltpu.VMEM((16, 64, 768), f32),
            pltpu.VMEM((CH, 8, 256), f32),
            pltpu.VMEM((CH, 8, 256), f32),
            pltpu.VMEM((16, 128), jnp.int32),
            pltpu.VMEM((CH, 256, 512), bf16),
            pltpu.VMEM((CH, 256, 512), bf16),
            pltpu.VMEM((CH, 256, 1024), f32),
            pltpu.VMEM((CH, 256, 1024), bf16),
            pltpu.VMEM((CH, 256, 1024), bf16),
            pltpu.VMEM((CH, 256, 512), bf16),
            pltpu.VMEM((CH, 256, 512), bf16),
            pltpu.VMEM((CH, 128, 512), bf16),
            pltpu.VMEM((8, CH, 128, 512), bf16),
            pltpu.VMEM((CH, 128, 4096), bf16),
            pltpu.SemaphoreType.DMA((17, CH)),
            pltpu.SemaphoreType.DMA((17, CH)),
            pltpu.SemaphoreType.DMA((12,)),
            pltpu.SemaphoreType.DMA((CH,)),
            pltpu.SemaphoreType.DMA((CH, 3)),
        ],
        compiler_params=pltpu.CompilerParams(
            collective_id=0, has_side_effects=True, vmem_limit_bytes=58 * 2**20
        ),
    )(
        pairing[0], lens, attn_gain.reshape(2, 1, 2048), ffn_gain.reshape(1, 4096),
        jnp.asarray(np.cos(angles), f32), jnp.asarray(np.sin(angles), f32), jnp.asarray(freq),
        candidates[0], w_query, w_key, w_value, w_out,
    )
    return resid[None], normed[None]


def solution(mesh):
    plane = mesh.shape["fsdp"] == 2 and mesh.shape["tensor"] == 4
    return jax.shard_map(
        on_plane if plane else on_device,
        mesh=mesh,
        in_specs=(
            P("dp", "fsdp", None, "tensor"),
            P("dp", "fsdp"),
            P("dp", None, None),
            P(),
            P("fsdp", "tensor"),
            P("fsdp", "tensor"),
            P("fsdp", "tensor"),
            P("tensor", "fsdp"),
            P(),
        ),
        out_specs=(P("dp", "fsdp", None, "tensor"), P("dp", "fsdp", None, None)),
        check_vma=False,
    )
```

```python
import jax
import jax.numpy as jnp
import numpy as np
from jax import lax
from jax.experimental import pallas as pl
from jax.experimental.pallas import tpu as pltpu
from jax.sharding import PartitionSpec as P

HEAD = 128


epsilon = 1e-05
rope_base = 500000.0


def rms_scale(values, gain):
    mean_square = jnp.mean(values * values, axis=-1, keepdims=True)
    return values * lax.rsqrt(mean_square + epsilon) * gain


def positions_of(lengths, sample):
    slot_steps = jnp.arange(2 * sample, dtype=jnp.int32)
    return jnp.where(slot_steps < sample, slot_steps, lengths[..., :1] + slot_steps - sample)


def key_mask(lengths, sample):
    slot_steps = jnp.arange(2 * sample, dtype=jnp.int32)
    local_step = jnp.where(slot_steps < sample, slot_steps, slot_steps - sample)
    limit = jnp.where(slot_steps < sample, lengths[..., :1], lengths[..., 1:])
    valid = local_step < limit
    causal = slot_steps[None, :] <= slot_steps[:, None]
    return causal[None] & valid[:, None, :]


def rotate(values, positions, head_size):
    half = head_size // 2
    inv_freq = rope_base ** (-jnp.arange(half, dtype=jnp.float32) * 2.0 / head_size)
    angles = positions.astype(jnp.float32)[..., None] * inv_freq
    cosine = jnp.cos(angles)[..., None, :]
    sine_table = jnp.sin(angles)[..., None, :]
    lower = values[..., :half]
    upper = values[..., half:]
    return jnp.concatenate(
        [lower * cosine - upper * sine_table, upper * cosine + lower * sine_table], axis=-1
    )


def attend(query, key_rows, value_rows, allowed):
    pair_rows, row_count, kv_count, group_size, head_size = query.shape
    scores = jnp.einsum(
        "bqkgd,bskd->bkgqs", query, key_rows, preferred_element_type=jnp.float32
    ) * head_size ** (-0.5)
    scores = jnp.where(allowed[:, None, None], scores, -1e30)
    row_peak = jnp.max(scores, axis=-1, keepdims=True)
    weights = jnp.exp(scores - row_peak)
    prob_rows = (weights / jnp.sum(weights, axis=-1, keepdims=True)).astype(jnp.bfloat16)
    mixed_rows = jnp.einsum(
        "bkgqs,bskd->bqkgd", prob_rows, value_rows, preferred_element_type=jnp.float32
    )
    return mixed_rows.astype(jnp.bfloat16).reshape(
        pair_rows * row_count, kv_count * group_size * head_size
    )


def on_device(
    candidates, cand_lengths, pairing, attn_gain, w_query, w_key, w_value, w_out, ffn_gain
):
    fsdp_count = lax.axis_size("fsdp")
    my_index = lax.axis_index("fsdp")
    cand_dev = candidates.shape[1]
    sample = candidates.shape[2]
    share_width = candidates.shape[3]
    pair_dev = cand_dev // 2
    most_slots = max(1, cand_dev // fsdp_count)
    flat_slots = pairing[0].reshape(-1)
    slot_count = flat_slots.shape[0]
    every_slot = jnp.arange(slot_count, dtype=jnp.int32)
    matches = flat_slots[:, None] == every_slot[None, :]
    target_slot = jnp.sum(jnp.where(matches, every_slot[:, None], 0), axis=0)
    target_dev = target_slot // cand_dev
    source_dev = every_slot // cand_dev
    earlier = (
        (source_dev[:, None] == source_dev[None, :])
        & (target_dev[:, None] == target_dev[None, :])
        & (every_slot[None, :] < every_slot[:, None])
    )
    send_rank = jnp.sum(earlier.astype(jnp.int32), axis=1)
    place = target_dev * most_slots + send_rank
    arrive = source_dev * most_slots + send_rank
    own_cands = my_index * cand_dev + jnp.arange(cand_dev, dtype=jnp.int32)
    own_pick = own_cands[:, None] == every_slot[None, :]
    own_place = jnp.sum(jnp.where(own_pick, place[None, :], 0), axis=1)
    buffer_slots = jnp.arange(fsdp_count * most_slots, dtype=jnp.int32)
    sender = buffer_slots[:, None] == own_place[None, :]
    outgoing = jnp.einsum(
        "bc,csf->bsf",
        sender.astype(jnp.bfloat16),
        candidates[0],
        preferred_element_type=jnp.float32,
    ).astype(jnp.bfloat16)
    out_lengths = jnp.sum(jnp.where(sender, cand_lengths[0][None, :], 0), axis=1)
    incoming, in_lengths = (
        lax.all_to_all(
            outgoing.reshape(fsdp_count, most_slots, sample, share_width),
            "fsdp",
            split_axis=0,
            concat_axis=0,
            tiled=True,
        ),
        lax.all_to_all(
            out_lengths.reshape(fsdp_count, most_slots),
            "fsdp",
            split_axis=0,
            concat_axis=0,
            tiled=True,
        ),
    )
    slot_pick = own_cands[:, None] == every_slot[None, :]
    wanted = jnp.sum(jnp.where(slot_pick, flat_slots[None, :], 0), axis=1)
    wanted_pick = wanted[:, None] == every_slot[None, :]
    wanted_from = jnp.sum(jnp.where(wanted_pick, arrive[None, :], 0), axis=1)
    receiver = wanted_from[:, None] == buffer_slots[None, :]
    local_rows = jnp.einsum(
        "cb,bsf->csf",
        receiver.astype(jnp.bfloat16),
        incoming.reshape(-1, sample, share_width),
        preferred_element_type=jnp.float32,
    ).astype(jnp.bfloat16)
    row_lengths = (
        jnp.sum(jnp.where(receiver, in_lengths.reshape(-1)[None, :], 0), axis=1)
        .astype(jnp.int32)
        .reshape(pair_dev, 2)
    )
    full_rows = lax.all_gather(local_rows, "tensor", axis=2, tiled=True)
    width = full_rows.shape[2]
    tok_count = cand_dev * sample
    inputs = full_rows.reshape(tok_count, width).astype(jnp.float32)
    normal_rows = rms_scale(inputs, attn_gain).astype(jnp.bfloat16)
    query_cols = w_query.shape[1]
    key_cols = w_key.shape[1]
    query = jnp.dot(
        normal_rows,
        lax.all_gather(w_query, "fsdp", axis=0, tiled=True),
        preferred_element_type=jnp.float32,
    )
    key_rows = jnp.dot(
        normal_rows,
        lax.all_gather(w_key, "fsdp", axis=0, tiled=True),
        preferred_element_type=jnp.float32,
    )
    value_rows = jnp.dot(
        normal_rows,
        lax.all_gather(w_value, "fsdp", axis=0, tiled=True),
        preferred_element_type=jnp.float32,
    )
    heads_here = query_cols // HEAD
    kv_here = key_cols // HEAD
    positions = positions_of(row_lengths, sample)
    query = rotate(query.reshape(pair_dev, 2 * sample, heads_here, HEAD), positions, HEAD).astype(
        jnp.bfloat16
    )
    key_rows = rotate(
        key_rows.reshape(pair_dev, 2 * sample, kv_here, HEAD), positions, HEAD
    ).astype(jnp.bfloat16)
    value_rows = value_rows.astype(jnp.bfloat16).reshape(pair_dev, 2 * sample, kv_here, HEAD)
    query = query.reshape(pair_dev, 2 * sample, kv_here, heads_here // kv_here, HEAD)
    mixed = attend(query, key_rows, value_rows, key_mask(row_lengths, sample))
    branch = jnp.dot(
        mixed, lax.all_gather(w_out, "fsdp", axis=1, tiled=True), preferred_element_type=jnp.float32
    )
    tensor_offset = lax.axis_index("tensor") * share_width
    summed_branch = lax.psum(branch.astype(jnp.bfloat16), "tensor").astype(jnp.float32)
    stream = inputs + summed_branch
    normed = rms_scale(stream, ffn_gain).astype(jnp.bfloat16)
    resid = lax.dynamic_slice_in_dim(stream, tensor_offset, share_width, 1).astype(jnp.bfloat16)
    return (
        resid.reshape(1, pair_dev, 2 * sample, share_width),
        normed.reshape(1, pair_dev, 2 * sample, width),
    )


MESH = pl.DeviceIdType.MESH
CH = 4
X1, Y1, Y2, S1A, S1B, S1C, XQ, XS, XM, SB, YB, XR, YR1, YR2, SR0, SR1, SR2, SR3, LN = range(19)
KINDS = 19


def plane_kernel(
    pair_ref, lens_ref, gain1_ref, cos_ref, sin_ref, freq_ref,
    cand_ref, wq_ref, wk_ref, wv_ref, wo_ref,
    stream_ref,
    grid_x, relay, lhs, w_in, w_out, q_send, q_recv, q_own, ss_own, ss_recv, own_lens, lens_all,
    mix_own, mix_recv, acc_own, sib_send, sib_recv, y_send, y_recv, x_send, stream,
    send_sem, recv_sem, load_sem, local_sem, store_sem,
):
    f = lax.axis_index("fsdp")
    t = lax.axis_index("tensor")
    y = t // 2
    c = t % 2
    x_dev = {"fsdp": 1 - f}
    t_y = (t + 2) % 4
    t_s = t + 1 - 2 * c
    t_sy = (t_s + 2) % 4
    y_dev = {"tensor": t_y}
    s_dev = {"tensor": t_s}
    even = f == y

    def remote(kind, j, src, dst, dev):
        return pltpu.make_async_remote_copy(
            src_ref=src, dst_ref=dst, send_sem=send_sem.at[kind, j],
            recv_sem=recv_sem.at[kind, j], device_id=dev, device_id_type=MESH,
        )

    loads = []

    def load(src, dst):
        copy = pltpu.make_async_copy(src, dst, load_sem.at[len(loads)])
        copy.start()
        loads.append(copy)

    mine = pl.multiple_of(f * 512, 512)
    other = pl.multiple_of((1 - f) * 512, 512)
    load(wq_ref.at[:, pl.ds(mine, 512)], w_in.at[:, 0:512])
    load(wq_ref.at[:, pl.ds(other, 512)], w_in.at[:, 512:1024])
    load(wk_ref, w_in.at[:, 1024:1152])
    load(wv_ref, w_in.at[:, 1152:1280])
    for r, row in enumerate((mine, other)):
        for b, block in enumerate((t, t_y, t_s, t_sy)):
            load(
                wo_ref.at[pl.ds(row, 512), pl.ds(pl.multiple_of(block * 512, 512), 512)],
                w_out.at[r * 512:(r + 1) * 512, b * 512:(b + 1) * 512],
            )

    barrier = pltpu.get_barrier_semaphore()
    for dev in (x_dev, y_dev, s_dev):
        pl.semaphore_signal(barrier, inc=1, device_id=dev, device_id_type=MESH)
    pl.semaphore_wait(barrier, 3)

    spread = jnp.broadcast_to(lens_ref[...].astype(jnp.float32), (8, 8))
    pick = lax.broadcasted_iota(jnp.int32, (8, 8), 0) == lax.broadcasted_iota(jnp.int32, (8, 8), 1)
    column = jnp.sum(jnp.where(pick, spread, 0.0), axis=1, keepdims=True)
    own_lens[...] = jnp.broadcast_to(column, (8, 128)).astype(jnp.int32)
    lens_copy = remote(LN, 0, own_lens, lens_all.at[pl.ds(pl.multiple_of(f * 8, 8), 8)], x_dev)
    lens_copy.start()
    lens_all[pl.ds(pl.multiple_of(f * 8, 8), 8), :] = own_lens[...]

    cols = pl.ds(pl.multiple_of(c * 1024, 1024), 1024)

    def place(g, j, at=0, count=2):
        return grid_x.at[pl.ds(g * 8 + 2 * j + at, count), :, cols]

    def own(j, at=0, count=2):
        return cand_ref.at[2 * j + at:2 * j + at + count]

    def hop(j):
        return relay.at[j:j + 1]

    def local_copy(j):
        return pltpu.make_async_copy(own(j), place(f, j), local_sem.at[j])

    def send_y(j):
        @pl.when(even)
        def _():
            remote(Y1, j, own(j), place(f, j), y_dev).start()

        @pl.when(jnp.logical_not(even))
        def _():
            remote(Y1, j, own(j, 1, 1), hop(j), y_dev).start()

    def far_x(j, at):
        return place(1 - f, j, at, 1)

    def forward_x(j):
        @pl.when(even)
        def _():
            remote(Y1, j, own(j, 1, 1), hop(j), y_dev).wait_recv()
            remote(X1, j, hop(j), place(f, j, 1, 1), x_dev).start()

    def forward_y(j):
        @pl.when(even)
        def _():
            remote(X1, j, own(j, 0, 1), far_x(j, 0), x_dev).wait_recv()
            remote(Y2, j, far_x(j, 0), far_x(j, 0), y_dev).start()
            remote(S1B, j, far_x(j, 0), far_x(j, 0), s_dev).start()
            local_copy(j).wait()

        @pl.when(jnp.logical_not(even))
        def _():
            remote(X1, j, hop(j), far_x(j, 1), x_dev).wait_recv()
            remote(Y2, j, far_x(j, 1), far_x(j, 1), y_dev).start()
            remote(S1B, j, far_x(j, 1), far_x(j, 1), s_dev).start()
            remote(Y1, j, own(j), place(f, j), y_dev).wait_recv()

        remote(S1A, j, place(f, j), place(f, j), s_dev).start()

    def finish_input(j):
        def last(at):
            remote(Y2, j, far_x(j, at), far_x(j, at), y_dev).wait_recv()
            remote(S1C, j, far_x(j, at), far_x(j, at), s_dev).start()
            remote(S1B, j, far_x(j, 1 - at), far_x(j, 1 - at), s_dev).wait_recv()
            remote(S1C, j, far_x(j, at), far_x(j, at), s_dev).wait_recv()

        @pl.when(even)
        def _():
            last(1)

        @pl.when(jnp.logical_not(even))
        def _():
            last(0)

        remote(S1A, j, place(f, j), place(f, j), s_dev).wait_recv()

    send_y(0)

    @pl.when(jnp.logical_not(even))
    def _():
        for j in range(CH):
            remote(X1, j, own(j, 0, 1), place(f, j, 0, 1), x_dev).start()

    send_y(1)

    @pl.when(even)
    def _():
        for j in range(CH):
            local_copy(j).start()

    for copy in loads[:4]:
        copy.wait()

    def finish(j):
        remote(XQ, j, q_send.at[j], q_recv.at[j], x_dev).wait_recv()
        remote(XS, j, ss_own.at[j], ss_recv.at[j], x_dev).wait_recv()
        total = (ss_own[j] + ss_recv[j])[0:1, :]
        scale = lax.rsqrt(total * (1.0 / 4096.0) + epsilon)
        column = jnp.broadcast_to(scale, (128, 256)).T
        for m in range(6):
            part = slice(m * 128, (m + 1) * 128)
            summed = q_own[4 * j:4 * j + 4, :, part].reshape(256, 128) + q_recv[
                j, :, part
            ].astype(jnp.float32)
            q_own[4 * j:4 * j + 4, :, part] = (summed * column).reshape(4, 64, 128)

    forward_x(0)
    for j in range(CH):
        forward_y(j)
        if j + 1 < CH:
            forward_x(j + 1)
        if j + 2 < CH:
            send_y(j + 2)
        finish_input(j)

        gain = gain1_ref[f]
        for g in range(2):
            values = grid_x[g * 8 + 2 * j:g * 8 + 2 * j + 2].reshape(128, 2048).astype(jnp.float32)
            squares = jnp.sum(values * values, axis=1, keepdims=True)
            ss_own[j, :, g * 128:(g + 1) * 128] = jnp.broadcast_to(squares, (128, 128)).T[0:8]
            lhs[g * 128:(g + 1) * 128, :] = (values * gain).astype(jnp.bfloat16)

        def project(n):
            return jnp.dot(
                lhs[...],
                w_in[:, pl.ds(pl.multiple_of(n * 256, 256), 256)],
                preferred_element_type=jnp.float32,
            )

        @pl.loop(0, 3)
        def _(n):
            result = project(n + 2)
            at = pl.ds(pl.multiple_of(n * 256, 256), 256)
            q_send[j, :, at] = result.astype(jnp.bfloat16)

        q_own[4 * j:4 * j + 4, :, 512:768] = project(4).reshape(4, 64, 256)
        remote(XQ, j, q_send.at[j], q_recv.at[j], x_dev).start()
        remote(XS, j, ss_own.at[j], ss_recv.at[j], x_dev).start()

        @pl.loop(0, 2)
        def _(n):
            result = project(n)
            at = pl.ds(pl.multiple_of(n * 256, 256), 256)
            q_own[4 * j:4 * j + 4, :, at] = result.reshape(4, 64, 256)

        if j > 1:
            finish(j - 2)
    finish(CH - 2)
    finish(CH - 1)
    lens_copy.wait()

    lane = lax.broadcasted_iota(jnp.int32, (1, 128), 1)
    sign = jnp.where(lane < 64, -1.0, 1.0)
    slot_t = lax.broadcasted_iota(jnp.int32, (128, 128), 0)
    slot_u = lax.broadcasted_iota(jnp.int32, (128, 128), 1)

    def packed(cand):
        return ((cand % 8) // 2) * 4 + (cand // 8) * 2 + cand % 2

    def attention(k, half):
        row = half * 4 + k
        cand0, cand1 = pair_ref[row, 0], pair_ref[row, 1]
        at0, at1 = packed(cand0), packed(cand1)
        len0 = lens_all[pl.ds(cand0, 1), :]
        len1 = lens_all[pl.ds(cand1, 1), :]
        angle = len0.astype(jnp.float32) * freq_ref[...]
        shift_cos, shift_sin = jnp.cos(angle), jnp.sin(angle)
        cos0, sin0 = cos_ref[...], sin_ref[...]
        cosine = jnp.concatenate([cos0, cos0 * shift_cos - sin0 * shift_sin], axis=0)
        sine = jnp.concatenate([sin0, sin0 * shift_cos + cos0 * shift_sin], axis=0) * sign
        allowed = (slot_u <= slot_t) & (lane < jnp.where(lane < 64, len0, len1 + 64))

        def block(m):
            part = slice(m * 128, (m + 1) * 128)
            return jnp.concatenate([q_own[at0, :, part], q_own[at1, :, part]], axis=0)

        def turned(m):
            values = block(m)
            return (values * cosine + pltpu.roll(values, 64, axis=1) * sine).astype(jnp.bfloat16)

        keys = turned(4)
        value_rows = block(5).astype(jnp.bfloat16)
        for h in range(4):
            scores = lax.dot_general(
                turned(h), keys, (((1,), (1,)), ((), ())), preferred_element_type=jnp.float32
            ) * HEAD ** (-0.5)
            scores = jnp.where(allowed, scores, -1e30)
            weights = jnp.exp(scores - jnp.max(scores, axis=1, keepdims=True))
            probs = weights / jnp.sum(weights, axis=1, keepdims=True)
            mixed = jnp.dot(
                probs.astype(jnp.bfloat16), value_rows, preferred_element_type=jnp.float32
            )
            mix_own[k, half * 128:(half + 1) * 128, h * 128:(h + 1) * 128] = mixed.astype(
                jnp.bfloat16
            )

    def stream_at(block, k):
        return stream.at[block, k]

    def own_block(k):
        return stream_at(f * 4 + t, k)

    def far_block(k):
        return stream_at((1 - f) * 4 + t, k)

    def share(kind, ref, k, dev):
        return remote(kind, k, ref, ref, dev)

    def mix_copy(k):
        return remote(XM, k, mix_own.at[k], mix_recv.at[k], x_dev)

    def partial_copy(k):
        return remote(SB, k, sib_send.at[k], sib_recv.at[k], s_dev)

    def pair_copy(k):
        return remote(YB, k, y_send.at[k], y_recv.at[k], y_dev)

    def cross_copy(k):
        return remote(XR, k, x_send.at[k], own_block(k), x_dev)

    def project_out(k):
        mix_copy(k).wait_recv()

        def term(n):
            at = pl.ds(pl.multiple_of(n * 256, 256), 256)
            return jnp.dot(
                mix_own[k], w_out[0:512, at], preferred_element_type=jnp.float32
            ) + jnp.dot(mix_recv[k], w_out[512:1024, at], preferred_element_type=jnp.float32)

        @pl.loop(0, 4)
        def _(n):
            at = pl.ds(pl.multiple_of(n * 256, 256), 256)
            sib_send[k, :, at] = term(n + 4).astype(jnp.bfloat16)

        partial_copy(k).start()

        @pl.loop(0, 4)
        def _(n):
            acc_own[k, :, pl.ds(pl.multiple_of(n * 256, 256), 256)] = term(n)

    def add_sibling(k):
        partial_copy(k).wait_recv()
        y_send[k] = (acc_own[k, :, 512:] + sib_recv[k, :, 512:].astype(jnp.float32)).astype(
            jnp.bfloat16
        )
        pair_copy(k).start()
        acc_own[k, :, 0:512] = acc_own[k, :, 0:512] + sib_recv[k, :, 0:512].astype(jnp.float32)

    def add_rows(k):
        pair_copy(k).wait_recv()
        at = pl.ds(pl.multiple_of(t * 512, 512), 512)
        parts = []
        for half in range(2):
            row = half * 4 + k
            rows = jnp.concatenate(
                [grid_x[pair_ref[row, 0], :, at], grid_x[pair_ref[row, 1], :, at]], axis=0
            )
            part = slice(half * 128, (half + 1) * 128)
            branch = acc_own[k, part, 0:512] + y_recv[k, part, :].astype(jnp.float32)
            parts.append(rows.astype(jnp.float32) + branch)
        first = f == 0
        x_send[k] = jnp.where(first, parts[1], parts[0]).astype(jnp.bfloat16)
        cross_copy(k).start()
        stream[f * 4 + t, k] = jnp.where(first, parts[0], parts[1]).astype(jnp.bfloat16)
        share(YR1, own_block(k), k, y_dev).start()
        share(SR0, own_block(k), k, s_dev).start()

    def pass_far(k):
        remote(XR, k, x_send.at[k], far_block(k), x_dev).wait_recv()
        share(YR2, far_block(k), k, y_dev).start()
        share(SR1, far_block(k), k, s_dev).start()

    def pass_pair(k):
        near = stream_at(f * 4 + t_y, k)
        far = stream_at((1 - f) * 4 + t_y, k)
        share(YR1, near, k, y_dev).wait_recv()
        share(SR2, near, k, s_dev).start()
        share(YR2, far, k, y_dev).wait_recv()
        share(SR3, far, k, s_dev).start()

    def store_copy(k):
        return pltpu.make_async_copy(stream.at[:, k], stream_ref.at[:, k], store_sem.at[k])

    def store(k):
        share(SR0, stream_at(f * 4 + t_s, k), k, s_dev).wait_recv()
        share(SR1, stream_at((1 - f) * 4 + t_s, k), k, s_dev).wait_recv()
        share(SR2, stream_at(f * 4 + t_sy, k), k, s_dev).wait_recv()
        share(SR3, stream_at((1 - f) * 4 + t_sy, k), k, s_dev).wait_recv()
        store_copy(k).start()

    for copy in loads[4:]:
        copy.wait()
    def attend_rows(k):
        attention(k, 0)
        attention(k, 1)
        mix_copy(k).start()

    attend_rows(0)
    attend_rows(1)
    attend_rows(2)
    project_out(0)
    attend_rows(3)
    add_sibling(0)
    project_out(1)
    add_sibling(1)
    add_rows(0)
    project_out(2)
    add_sibling(2)
    add_rows(1)
    pass_far(0)
    project_out(3)
    add_sibling(3)
    add_rows(2)
    pass_far(1)
    pass_pair(0)
    add_rows(3)
    pass_far(2)
    pass_pair(1)
    store(0)
    pass_far(3)
    pass_pair(2)
    store(1)
    pass_pair(3)
    store(2)
    store(3)

    for j in range(CH):

        @pl.when(even)
        def _():
            remote(Y1, j, own(j), place(f, j), y_dev).wait_send()
            remote(X1, j, hop(j), place(f, j, 1, 1), x_dev).wait_send()
            remote(Y2, j, far_x(j, 0), far_x(j, 0), y_dev).wait_send()
            remote(S1B, j, far_x(j, 0), far_x(j, 0), s_dev).wait_send()
            remote(S1C, j, far_x(j, 1), far_x(j, 1), s_dev).wait_send()

        @pl.when(jnp.logical_not(even))
        def _():
            remote(Y1, j, own(j, 1, 1), hop(j), y_dev).wait_send()
            remote(X1, j, own(j, 0, 1), place(f, j, 0, 1), x_dev).wait_send()
            remote(Y2, j, far_x(j, 1), far_x(j, 1), y_dev).wait_send()
            remote(S1B, j, far_x(j, 1), far_x(j, 1), s_dev).wait_send()
            remote(S1C, j, far_x(j, 0), far_x(j, 0), s_dev).wait_send()

        remote(S1A, j, place(f, j), place(f, j), s_dev).wait_send()
        remote(XQ, j, q_send.at[j], q_recv.at[j], x_dev).wait_send()
        remote(XS, j, ss_own.at[j], ss_recv.at[j], x_dev).wait_send()
        mix_copy(j).wait_send()
        partial_copy(j).wait_send()
        pair_copy(j).wait_send()
        cross_copy(j).wait_send()
        share(YR1, own_block(j), j, y_dev).wait_send()
        share(SR0, own_block(j), j, s_dev).wait_send()
        share(YR2, far_block(j), j, y_dev).wait_send()
        share(SR1, far_block(j), j, s_dev).wait_send()
        share(SR2, stream_at(f * 4 + t_y, j), j, s_dev).wait_send()
        share(SR3, stream_at((1 - f) * 4 + t_y, j), j, s_dev).wait_send()
        store_copy(j).wait()


def norm_kernel(stream_ref, gain2_ref, resid_ref, normed_ref):
    t = lax.axis_index("tensor")
    squares = jnp.zeros((128, 512), jnp.float32)
    for b in range(8):
        values = stream_ref[b, 0].astype(jnp.float32)
        squares = squares + values * values
    scale = lax.rsqrt(jnp.sum(squares, axis=1, keepdims=True) * (1.0 / 4096.0) + epsilon)
    for b in range(8):
        part = slice(b * 512, (b + 1) * 512)
        normed_ref[0, :, part] = (
            stream_ref[b, 0].astype(jnp.float32) * scale * gain2_ref[:, part]
        ).astype(jnp.bfloat16)
    resid_ref[0, :, 0:512] = stream_ref[2 * t, 0]
    resid_ref[0, :, 512:1024] = stream_ref[2 * t + 1, 0]


def on_plane(
    candidates, cand_lengths, pairing, attn_gain, w_query, w_key, w_value, w_out, ffn_gain
):
    half = HEAD // 2
    inv_freq = np.float32(rope_base) ** (-np.arange(half, dtype=np.float32) * 2.0 / HEAD)
    freq = np.concatenate([inv_freq, inv_freq]).astype(np.float32)[None, :]
    angles = (np.arange(64, dtype=np.float32)[:, None] * freq).astype(np.float64)
    bf16, f32 = jnp.bfloat16, jnp.float32
    vmem = pl.BlockSpec(memory_space=pltpu.VMEM)
    hbm = pl.BlockSpec(memory_space=pl.ANY)
    stream = pl.pallas_call(
        plane_kernel,
        out_shape=jax.ShapeDtypeStruct((8, CH, 128, 512), bf16),
        in_specs=[pl.BlockSpec(memory_space=pltpu.SMEM)] + [vmem] * 5 + [hbm] * 5,
        out_specs=hbm,
        scratch_shapes=[
            pltpu.VMEM((16, 64, 2048), bf16),
            pltpu.VMEM((CH, 64, 1024), bf16),
            pltpu.VMEM((256, 2048), bf16),
            pltpu.VMEM((2048, 1280), bf16),
            pltpu.VMEM((1024, 2048), bf16),
            pltpu.VMEM((CH, 256, 768), bf16),
            pltpu.VMEM((CH, 256, 768), bf16),
            pltpu.VMEM((16, 64, 768), f32),
            pltpu.VMEM((CH, 8, 256), f32),
            pltpu.VMEM((CH, 8, 256), f32),
            pltpu.VMEM((8, 128), jnp.int32),
            pltpu.VMEM((16, 128), jnp.int32),
            pltpu.VMEM((CH, 256, 512), bf16),
            pltpu.VMEM((CH, 256, 512), bf16),
            pltpu.VMEM((CH, 256, 1024), f32),
            pltpu.VMEM((CH, 256, 1024), bf16),
            pltpu.VMEM((CH, 256, 1024), bf16),
            pltpu.VMEM((CH, 256, 512), bf16),
            pltpu.VMEM((CH, 256, 512), bf16),
            pltpu.VMEM((CH, 128, 512), bf16),
            pltpu.VMEM((8, CH, 128, 512), bf16),
            pltpu.SemaphoreType.DMA((KINDS, CH)),
            pltpu.SemaphoreType.DMA((KINDS, CH)),
            pltpu.SemaphoreType.DMA((12,)),
            pltpu.SemaphoreType.DMA((CH,)),
            pltpu.SemaphoreType.DMA((CH,)),
        ],
        compiler_params=pltpu.CompilerParams(
            collective_id=0, has_side_effects=True, vmem_limit_bytes=58 * 2**20
        ),
    )(
        pairing[0], cand_lengths, attn_gain.reshape(2, 1, 2048),
        jnp.asarray(np.cos(angles), f32), jnp.asarray(np.sin(angles), f32), jnp.asarray(freq),
        candidates[0], w_query, w_key, w_value, w_out,
    )
    resid, normed = pl.pallas_call(
        norm_kernel,
        grid=(CH,),
        out_shape=(
            jax.ShapeDtypeStruct((CH, 128, 1024), bf16),
            jax.ShapeDtypeStruct((CH, 128, 4096), bf16),
        ),
        in_specs=[
            pl.BlockSpec((8, 1, 128, 512), lambda k: (0, k, 0, 0)),
            pl.BlockSpec((1, 4096), lambda k: (0, 0)),
        ],
        out_specs=(
            pl.BlockSpec((1, 128, 1024), lambda k: (k, 0, 0)),
            pl.BlockSpec((1, 128, 4096), lambda k: (k, 0, 0)),
        ),
        compiler_params=pltpu.CompilerParams(vmem_limit_bytes=32 * 2**20),
    )(stream, ffn_gain.reshape(1, 4096))
    return resid[None], normed[None]


def solution(mesh):
    plane = mesh.shape["fsdp"] == 2 and mesh.shape["tensor"] == 4
    return jax.shard_map(
        on_plane if plane else on_device,
        mesh=mesh,
        in_specs=(
            P("dp", "fsdp", None, "tensor"),
            P("dp", "fsdp"),
            P("dp", None, None),
            P(),
            P("fsdp", "tensor"),
            P("fsdp", "tensor"),
            P("fsdp", "tensor"),
            P("tensor", "fsdp"),
            P(),
        ),
        out_specs=(P("dp", "fsdp", None, "tensor"), P("dp", "fsdp", None, None)),
        check_vma=False,
    )
```

```python
import jax
import jax.numpy as jnp
import numpy as np
from jax import lax
from jax.experimental import pallas as pl
from jax.experimental.pallas import tpu as pltpu
from jax.sharding import PartitionSpec as P

HEAD = 128


epsilon = 1e-05
rope_base = 500000.0


def rms_scale(values, gain):
    mean_square = jnp.mean(values * values, axis=-1, keepdims=True)
    return values * lax.rsqrt(mean_square + epsilon) * gain


def positions_of(lengths, sample):
    slot_steps = jnp.arange(2 * sample, dtype=jnp.int32)
    return jnp.where(slot_steps < sample, slot_steps, lengths[..., :1] + slot_steps - sample)


def key_mask(lengths, sample):
    slot_steps = jnp.arange(2 * sample, dtype=jnp.int32)
    local_step = jnp.where(slot_steps < sample, slot_steps, slot_steps - sample)
    limit = jnp.where(slot_steps < sample, lengths[..., :1], lengths[..., 1:])
    valid = local_step < limit
    causal = slot_steps[None, :] <= slot_steps[:, None]
    return causal[None] & valid[:, None, :]


def rotate(values, positions, head_size):
    half = head_size // 2
    inv_freq = rope_base ** (-jnp.arange(half, dtype=jnp.float32) * 2.0 / head_size)
    angles = positions.astype(jnp.float32)[..., None] * inv_freq
    cosine = jnp.cos(angles)[..., None, :]
    sine_table = jnp.sin(angles)[..., None, :]
    lower = values[..., :half]
    upper = values[..., half:]
    return jnp.concatenate(
        [lower * cosine - upper * sine_table, upper * cosine + lower * sine_table], axis=-1
    )


def attend(query, key_rows, value_rows, allowed):
    pair_rows, row_count, kv_count, group_size, head_size = query.shape
    scores = jnp.einsum(
        "bqkgd,bskd->bkgqs", query, key_rows, preferred_element_type=jnp.float32
    ) * head_size ** (-0.5)
    scores = jnp.where(allowed[:, None, None], scores, -1e30)
    row_peak = jnp.max(scores, axis=-1, keepdims=True)
    weights = jnp.exp(scores - row_peak)
    prob_rows = (weights / jnp.sum(weights, axis=-1, keepdims=True)).astype(jnp.bfloat16)
    mixed_rows = jnp.einsum(
        "bkgqs,bskd->bqkgd", prob_rows, value_rows, preferred_element_type=jnp.float32
    )
    return mixed_rows.astype(jnp.bfloat16).reshape(
        pair_rows * row_count, kv_count * group_size * head_size
    )


def on_device(
    candidates, cand_lengths, pairing, attn_gain, w_query, w_key, w_value, w_out, ffn_gain
):
    fsdp_count = lax.axis_size("fsdp")
    my_index = lax.axis_index("fsdp")
    cand_dev = candidates.shape[1]
    sample = candidates.shape[2]
    share_width = candidates.shape[3]
    pair_dev = cand_dev // 2
    most_slots = max(1, cand_dev // fsdp_count)
    flat_slots = pairing[0].reshape(-1)
    slot_count = flat_slots.shape[0]
    every_slot = jnp.arange(slot_count, dtype=jnp.int32)
    matches = flat_slots[:, None] == every_slot[None, :]
    target_slot = jnp.sum(jnp.where(matches, every_slot[:, None], 0), axis=0)
    target_dev = target_slot // cand_dev
    source_dev = every_slot // cand_dev
    earlier = (
        (source_dev[:, None] == source_dev[None, :])
        & (target_dev[:, None] == target_dev[None, :])
        & (every_slot[None, :] < every_slot[:, None])
    )
    send_rank = jnp.sum(earlier.astype(jnp.int32), axis=1)
    place = target_dev * most_slots + send_rank
    arrive = source_dev * most_slots + send_rank
    own_cands = my_index * cand_dev + jnp.arange(cand_dev, dtype=jnp.int32)
    own_pick = own_cands[:, None] == every_slot[None, :]
    own_place = jnp.sum(jnp.where(own_pick, place[None, :], 0), axis=1)
    buffer_slots = jnp.arange(fsdp_count * most_slots, dtype=jnp.int32)
    sender = buffer_slots[:, None] == own_place[None, :]
    outgoing = jnp.einsum(
        "bc,csf->bsf",
        sender.astype(jnp.bfloat16),
        candidates[0],
        preferred_element_type=jnp.float32,
    ).astype(jnp.bfloat16)
    out_lengths = jnp.sum(jnp.where(sender, cand_lengths[0][None, :], 0), axis=1)
    incoming, in_lengths = (
        lax.all_to_all(
            outgoing.reshape(fsdp_count, most_slots, sample, share_width),
            "fsdp",
            split_axis=0,
            concat_axis=0,
            tiled=True,
        ),
        lax.all_to_all(
            out_lengths.reshape(fsdp_count, most_slots),
            "fsdp",
            split_axis=0,
            concat_axis=0,
            tiled=True,
        ),
    )
    slot_pick = own_cands[:, None] == every_slot[None, :]
    wanted = jnp.sum(jnp.where(slot_pick, flat_slots[None, :], 0), axis=1)
    wanted_pick = wanted[:, None] == every_slot[None, :]
    wanted_from = jnp.sum(jnp.where(wanted_pick, arrive[None, :], 0), axis=1)
    receiver = wanted_from[:, None] == buffer_slots[None, :]
    local_rows = jnp.einsum(
        "cb,bsf->csf",
        receiver.astype(jnp.bfloat16),
        incoming.reshape(-1, sample, share_width),
        preferred_element_type=jnp.float32,
    ).astype(jnp.bfloat16)
    row_lengths = (
        jnp.sum(jnp.where(receiver, in_lengths.reshape(-1)[None, :], 0), axis=1)
        .astype(jnp.int32)
        .reshape(pair_dev, 2)
    )
    full_rows = lax.all_gather(local_rows, "tensor", axis=2, tiled=True)
    width = full_rows.shape[2]
    tok_count = cand_dev * sample
    inputs = full_rows.reshape(tok_count, width).astype(jnp.float32)
    normal_rows = rms_scale(inputs, attn_gain).astype(jnp.bfloat16)
    query_cols = w_query.shape[1]
    key_cols = w_key.shape[1]
    query = jnp.dot(
        normal_rows,
        lax.all_gather(w_query, "fsdp", axis=0, tiled=True),
        preferred_element_type=jnp.float32,
    )
    key_rows = jnp.dot(
        normal_rows,
        lax.all_gather(w_key, "fsdp", axis=0, tiled=True),
        preferred_element_type=jnp.float32,
    )
    value_rows = jnp.dot(
        normal_rows,
        lax.all_gather(w_value, "fsdp", axis=0, tiled=True),
        preferred_element_type=jnp.float32,
    )
    heads_here = query_cols // HEAD
    kv_here = key_cols // HEAD
    positions = positions_of(row_lengths, sample)
    query = rotate(query.reshape(pair_dev, 2 * sample, heads_here, HEAD), positions, HEAD).astype(
        jnp.bfloat16
    )
    key_rows = rotate(
        key_rows.reshape(pair_dev, 2 * sample, kv_here, HEAD), positions, HEAD
    ).astype(jnp.bfloat16)
    value_rows = value_rows.astype(jnp.bfloat16).reshape(pair_dev, 2 * sample, kv_here, HEAD)
    query = query.reshape(pair_dev, 2 * sample, kv_here, heads_here // kv_here, HEAD)
    mixed = attend(query, key_rows, value_rows, key_mask(row_lengths, sample))
    branch = jnp.dot(
        mixed, lax.all_gather(w_out, "fsdp", axis=1, tiled=True), preferred_element_type=jnp.float32
    )
    tensor_offset = lax.axis_index("tensor") * share_width
    summed_branch = lax.psum(branch.astype(jnp.bfloat16), "tensor").astype(jnp.float32)
    stream = inputs + summed_branch
    normed = rms_scale(stream, ffn_gain).astype(jnp.bfloat16)
    resid = lax.dynamic_slice_in_dim(stream, tensor_offset, share_width, 1).astype(jnp.bfloat16)
    return (
        resid.reshape(1, pair_dev, 2 * sample, share_width),
        normed.reshape(1, pair_dev, 2 * sample, width),
    )


MESH = pl.DeviceIdType.MESH
CH = 4
PARTS = 8
X1, Y1, Y2, S1A, S1B, S1C, XQ, XS, XM, SB, YB, XR, YR1, YR2, SR0, SR1, SR2, SR3, LN = range(19)
KINDS = 19


def plane_kernel(
    pair_ref, lens_ref, gain1_ref, cos_ref, sin_ref, freq_ref,
    cand_ref, wq_ref, wk_ref, wv_ref, wo_ref,
    stream_ref,
    grid_x, relay, lhs, w_in, w_out, q_send, q_recv, q_own, ss_own, ss_recv, own_lens, lens_all,
    mix_own, mix_recv, acc_own, sib_send, sib_recv, y_send, y_recv, x_send, stream,
    send_sem, recv_sem, load_sem, local_sem, store_sem,
):
    f = lax.axis_index("fsdp")
    t = lax.axis_index("tensor")
    y = t // 2
    c = t % 2
    x_dev = {"fsdp": 1 - f}
    t_y = (t + 2) % 4
    t_s = t + 1 - 2 * c
    t_sy = (t_s + 2) % 4
    y_dev = {"tensor": t_y}
    s_dev = {"tensor": t_s}
    even = f == y

    def remote(kind, j, src, dst, dev):
        return pltpu.make_async_remote_copy(
            src_ref=src, dst_ref=dst, send_sem=send_sem.at[kind, j],
            recv_sem=recv_sem.at[kind, j], device_id=dev, device_id_type=MESH,
        )

    loads = []

    def load(src, dst):
        copy = pltpu.make_async_copy(src, dst, load_sem.at[len(loads)])
        copy.start()
        loads.append(copy)

    mine = pl.multiple_of(f * 512, 512)
    other = pl.multiple_of((1 - f) * 512, 512)
    load(wq_ref.at[:, pl.ds(mine, 512)], w_in.at[:, 0:512])
    load(wq_ref.at[:, pl.ds(other, 512)], w_in.at[:, 512:1024])
    load(wk_ref, w_in.at[:, 1024:1152])
    load(wv_ref, w_in.at[:, 1152:1280])
    for r, row in enumerate((mine, other)):
        for b, block in enumerate((t, t_y, t_s, t_sy)):
            load(
                wo_ref.at[pl.ds(row, 512), pl.ds(pl.multiple_of(block * 512, 512), 512)],
                w_out.at[r * 512:(r + 1) * 512, b * 512:(b + 1) * 512],
            )

    barrier = pltpu.get_barrier_semaphore()
    for dev in (x_dev, y_dev, s_dev):
        pl.semaphore_signal(barrier, inc=1, device_id=dev, device_id_type=MESH)
    pl.semaphore_wait(barrier, 3)

    spread = jnp.broadcast_to(lens_ref[...].astype(jnp.float32), (8, 8))
    pick = lax.broadcasted_iota(jnp.int32, (8, 8), 0) == lax.broadcasted_iota(jnp.int32, (8, 8), 1)
    column = jnp.sum(jnp.where(pick, spread, 0.0), axis=1, keepdims=True)
    own_lens[...] = jnp.broadcast_to(column, (8, 128)).astype(jnp.int32)
    lens_copy = remote(LN, 0, own_lens, lens_all.at[pl.ds(pl.multiple_of(f * 8, 8), 8)], x_dev)
    lens_copy.start()
    lens_all[pl.ds(pl.multiple_of(f * 8, 8), 8), :] = own_lens[...]

    cols = pl.ds(pl.multiple_of(c * 1024, 1024), 1024)

    def place(g, j, at=0, count=2):
        return grid_x.at[pl.ds(g * 8 + 2 * j + at, count), :, cols]

    def own(j, at=0, count=2):
        return cand_ref.at[2 * j + at:2 * j + at + count]

    def hop(j):
        return relay.at[j:j + 1]

    def local_copy(j):
        return pltpu.make_async_copy(own(j), place(f, j), local_sem.at[j])

    def send_y(j):
        @pl.when(even)
        def _():
            remote(Y1, j, own(j), place(f, j), y_dev).start()

        @pl.when(jnp.logical_not(even))
        def _():
            remote(Y1, j, own(j, 1, 1), hop(j), y_dev).start()

    def far_x(j, at):
        return place(1 - f, j, at, 1)

    def forward_x(j):
        @pl.when(even)
        def _():
            remote(Y1, j, own(j, 1, 1), hop(j), y_dev).wait_recv()
            remote(X1, j, hop(j), place(f, j, 1, 1), x_dev).start()

    def forward_y(j):
        @pl.when(even)
        def _():
            remote(X1, j, own(j, 0, 1), far_x(j, 0), x_dev).wait_recv()
            remote(Y2, j, far_x(j, 0), far_x(j, 0), y_dev).start()
            remote(S1B, j, far_x(j, 0), far_x(j, 0), s_dev).start()
            local_copy(j).wait()

        @pl.when(jnp.logical_not(even))
        def _():
            remote(X1, j, hop(j), far_x(j, 1), x_dev).wait_recv()
            remote(Y2, j, far_x(j, 1), far_x(j, 1), y_dev).start()
            remote(S1B, j, far_x(j, 1), far_x(j, 1), s_dev).start()
            remote(Y1, j, own(j), place(f, j), y_dev).wait_recv()

        remote(S1A, j, place(f, j), place(f, j), s_dev).start()

    def finish_input(j):
        def last(at):
            remote(Y2, j, far_x(j, at), far_x(j, at), y_dev).wait_recv()
            remote(S1C, j, far_x(j, at), far_x(j, at), s_dev).start()
            remote(S1B, j, far_x(j, 1 - at), far_x(j, 1 - at), s_dev).wait_recv()
            remote(S1C, j, far_x(j, at), far_x(j, at), s_dev).wait_recv()

        @pl.when(even)
        def _():
            last(1)

        @pl.when(jnp.logical_not(even))
        def _():
            last(0)

        remote(S1A, j, place(f, j), place(f, j), s_dev).wait_recv()

    send_y(0)

    @pl.when(jnp.logical_not(even))
    def _():
        for j in range(CH):
            remote(X1, j, own(j, 0, 1), place(f, j, 0, 1), x_dev).start()

    send_y(1)

    @pl.when(even)
    def _():
        for j in range(CH):
            local_copy(j).start()

    for copy in loads[:4]:
        copy.wait()

    def finish(j):
        remote(XQ, j, q_send.at[j], q_recv.at[j], x_dev).wait_recv()
        remote(XS, j, ss_own.at[j], ss_recv.at[j], x_dev).wait_recv()
        total = (ss_own[j] + ss_recv[j])[0:1, :]
        scale = lax.rsqrt(total * (1.0 / 4096.0) + epsilon)
        column = jnp.broadcast_to(scale, (128, 256)).T
        for m in range(6):
            part = slice(m * 128, (m + 1) * 128)
            summed = q_own[4 * j:4 * j + 4, :, part].reshape(256, 128) + q_recv[
                j, :, part
            ].astype(jnp.float32)
            q_own[4 * j:4 * j + 4, :, part] = (summed * column).reshape(4, 64, 128)

    forward_x(0)
    for j in range(CH):
        forward_y(j)
        if j + 1 < CH:
            forward_x(j + 1)
        if j + 2 < CH:
            send_y(j + 2)
        finish_input(j)

        gain = gain1_ref[f]
        for g in range(2):
            values = grid_x[g * 8 + 2 * j:g * 8 + 2 * j + 2].reshape(128, 2048).astype(jnp.float32)
            squares = jnp.sum(values * values, axis=1, keepdims=True)
            ss_own[j, :, g * 128:(g + 1) * 128] = jnp.broadcast_to(squares, (128, 128)).T[0:8]
            lhs[g * 128:(g + 1) * 128, :] = (values * gain).astype(jnp.bfloat16)

        def project(n):
            return jnp.dot(
                lhs[...],
                w_in[:, pl.ds(pl.multiple_of(n * 256, 256), 256)],
                preferred_element_type=jnp.float32,
            )

        @pl.loop(0, 3)
        def _(n):
            result = project(n + 2)
            at = pl.ds(pl.multiple_of(n * 256, 256), 256)
            q_send[j, :, at] = result.astype(jnp.bfloat16)

        q_own[4 * j:4 * j + 4, :, 512:768] = project(4).reshape(4, 64, 256)
        remote(XQ, j, q_send.at[j], q_recv.at[j], x_dev).start()
        remote(XS, j, ss_own.at[j], ss_recv.at[j], x_dev).start()

        @pl.loop(0, 2)
        def _(n):
            result = project(n)
            at = pl.ds(pl.multiple_of(n * 256, 256), 256)
            q_own[4 * j:4 * j + 4, :, at] = result.reshape(4, 64, 256)

        if j > 1:
            finish(j - 2)
    finish(CH - 2)
    finish(CH - 1)
    lens_copy.wait()

    lane = lax.broadcasted_iota(jnp.int32, (1, 128), 1)
    sign = jnp.where(lane < 64, -1.0, 1.0)
    slot_t = lax.broadcasted_iota(jnp.int32, (128, 128), 0)
    slot_u = lax.broadcasted_iota(jnp.int32, (128, 128), 1)

    def packed(cand):
        return ((cand % 8) // 2) * 4 + (cand // 8) * 2 + cand % 2

    def attention(k, half):
        row = half * 4 + k
        cand0, cand1 = pair_ref[row, 0], pair_ref[row, 1]
        at0, at1 = packed(cand0), packed(cand1)
        len0 = lens_all[pl.ds(cand0, 1), :]
        len1 = lens_all[pl.ds(cand1, 1), :]
        angle = len0.astype(jnp.float32) * freq_ref[...]
        shift_cos, shift_sin = jnp.cos(angle), jnp.sin(angle)
        cos0, sin0 = cos_ref[...], sin_ref[...]
        cosine = jnp.concatenate([cos0, cos0 * shift_cos - sin0 * shift_sin], axis=0)
        sine = jnp.concatenate([sin0, sin0 * shift_cos + cos0 * shift_sin], axis=0) * sign
        allowed = (slot_u <= slot_t) & (lane < jnp.where(lane < 64, len0, len1 + 64))

        def block(m):
            part = slice(m * 128, (m + 1) * 128)
            return jnp.concatenate([q_own[at0, :, part], q_own[at1, :, part]], axis=0)

        def turned(m):
            values = block(m)
            return (values * cosine + pltpu.roll(values, 64, axis=1) * sine).astype(jnp.bfloat16)

        keys = turned(4)
        value_rows = block(5).astype(jnp.bfloat16)
        queries = jnp.concatenate([turned(h) for h in range(4)], axis=0)
        scores = lax.dot_general(
            queries, keys, (((1,), (1,)), ((), ())), preferred_element_type=jnp.float32
        ) * HEAD ** (-0.5)
        scores = jnp.where(jnp.concatenate([allowed] * 4, axis=0), scores, -1e30)
        weights = jnp.exp(scores - jnp.max(scores, axis=1, keepdims=True))
        probs = weights * (1.0 / jnp.sum(weights, axis=1, keepdims=True))
        mixed = jnp.dot(
            probs.astype(jnp.bfloat16), value_rows, preferred_element_type=jnp.float32
        ).astype(jnp.bfloat16)
        for h in range(4):
            for s in range(2):
                mix_own[2 * k + s, half * 64:(half + 1) * 64, h * 128:(h + 1) * 128] = mixed[
                    h * 128 + s * 64:h * 128 + (s + 1) * 64
                ]

    def stream_at(block, k):
        return stream.at[block, k]

    def own_block(k):
        return stream_at(f * 4 + t, k)

    def far_block(k):
        return stream_at((1 - f) * 4 + t, k)

    def share(kind, ref, k, dev):
        return remote(kind, k, ref, ref, dev)

    def mix_copy(k):
        return remote(XM, k, mix_own.at[k], mix_recv.at[k], x_dev)

    def partial_copy(k):
        return remote(SB, k, sib_send.at[k], sib_recv.at[k], s_dev)

    def pair_copy(k):
        return remote(YB, k, y_send.at[k], y_recv.at[k], y_dev)

    def cross_copy(k):
        return remote(XR, k, x_send.at[k], own_block(k), x_dev)

    def project_out(k):
        mix_copy(k).wait_recv()

        def term(n):
            at = pl.ds(pl.multiple_of(n * 256, 256), 256)
            return jnp.dot(
                mix_own[k], w_out[0:512, at], preferred_element_type=jnp.float32
            ) + jnp.dot(mix_recv[k], w_out[512:1024, at], preferred_element_type=jnp.float32)

        @pl.loop(0, 4)
        def _(n):
            at = pl.ds(pl.multiple_of(n * 256, 256), 256)
            sib_send[k, :, at] = term(n + 4).astype(jnp.bfloat16)

        partial_copy(k).start()

        @pl.loop(0, 4)
        def _(n):
            acc_own[k, :, pl.ds(pl.multiple_of(n * 256, 256), 256)] = term(n)

    def add_sibling(k):
        partial_copy(k).wait_recv()
        y_send[k] = (acc_own[k, :, 512:] + sib_recv[k, :, 512:].astype(jnp.float32)).astype(
            jnp.bfloat16
        )
        pair_copy(k).start()
        acc_own[k, :, 0:512] = acc_own[k, :, 0:512] + sib_recv[k, :, 0:512].astype(jnp.float32)

    def add_rows(k):
        pair_copy(k).wait_recv()
        at = pl.ds(pl.multiple_of(t * 512, 512), 512)
        parts = []
        for half in range(2):
            rows = grid_x[pair_ref[half * 4 + k // 2, k % 2], :, at]
            part = slice(half * 64, (half + 1) * 64)
            branch = acc_own[k, part, 0:512] + y_recv[k, part, :].astype(jnp.float32)
            parts.append(rows.astype(jnp.float32) + branch)
        first = f == 0
        x_send[k] = jnp.where(first, parts[1], parts[0]).astype(jnp.bfloat16)
        cross_copy(k).start()
        stream[f * 4 + t, k] = jnp.where(first, parts[0], parts[1]).astype(jnp.bfloat16)
        share(YR1, own_block(k), k, y_dev).start()
        share(SR0, own_block(k), k, s_dev).start()

    def pass_far(k):
        remote(XR, k, x_send.at[k], far_block(k), x_dev).wait_recv()
        share(YR2, far_block(k), k, y_dev).start()
        share(SR1, far_block(k), k, s_dev).start()

    def pass_pair(k):
        near = stream_at(f * 4 + t_y, k)
        far = stream_at((1 - f) * 4 + t_y, k)
        share(YR1, near, k, y_dev).wait_recv()
        share(SR2, near, k, s_dev).start()
        share(YR2, far, k, y_dev).wait_recv()
        share(SR3, far, k, s_dev).start()

    def store_copy(k):
        return pltpu.make_async_copy(stream.at[:, k], stream_ref.at[:, k], store_sem.at[k])

    def store(k):
        share(SR0, stream_at(f * 4 + t_s, k), k, s_dev).wait_recv()
        share(SR1, stream_at((1 - f) * 4 + t_s, k), k, s_dev).wait_recv()
        share(SR2, stream_at(f * 4 + t_sy, k), k, s_dev).wait_recv()
        share(SR3, stream_at((1 - f) * 4 + t_sy, k), k, s_dev).wait_recv()
        store_copy(k).start()

    for copy in loads[4:]:
        copy.wait()
    def attend_rows(k):
        attention(k, 0)
        attention(k, 1)
        mix_copy(2 * k).start()
        mix_copy(2 * k + 1).start()

    order = [(2.0 * j - 2.5, attend_rows, j) for j in range(PARTS // 2)]
    for lag, stage in (
        (0.0, project_out), (0.8, add_sibling), (2.1, add_rows),
        (3.2, pass_far), (4.3, pass_pair), (5.4, store),
    ):
        order += [(k + lag, stage, k) for k in range(PARTS)]
    for _, stage, k in sorted(order, key=lambda item: item[0]):
        stage(k)

    for j in range(CH):

        @pl.when(even)
        def _():
            remote(Y1, j, own(j), place(f, j), y_dev).wait_send()
            remote(X1, j, hop(j), place(f, j, 1, 1), x_dev).wait_send()
            remote(Y2, j, far_x(j, 0), far_x(j, 0), y_dev).wait_send()
            remote(S1B, j, far_x(j, 0), far_x(j, 0), s_dev).wait_send()
            remote(S1C, j, far_x(j, 1), far_x(j, 1), s_dev).wait_send()

        @pl.when(jnp.logical_not(even))
        def _():
            remote(Y1, j, own(j, 1, 1), hop(j), y_dev).wait_send()
            remote(X1, j, own(j, 0, 1), place(f, j, 0, 1), x_dev).wait_send()
            remote(Y2, j, far_x(j, 1), far_x(j, 1), y_dev).wait_send()
            remote(S1B, j, far_x(j, 1), far_x(j, 1), s_dev).wait_send()
            remote(S1C, j, far_x(j, 0), far_x(j, 0), s_dev).wait_send()

        remote(S1A, j, place(f, j), place(f, j), s_dev).wait_send()
        remote(XQ, j, q_send.at[j], q_recv.at[j], x_dev).wait_send()
        remote(XS, j, ss_own.at[j], ss_recv.at[j], x_dev).wait_send()
    for j in range(PARTS):
        mix_copy(j).wait_send()
        partial_copy(j).wait_send()
        pair_copy(j).wait_send()
        cross_copy(j).wait_send()
        share(YR1, own_block(j), j, y_dev).wait_send()
        share(SR0, own_block(j), j, s_dev).wait_send()
        share(YR2, far_block(j), j, y_dev).wait_send()
        share(SR1, far_block(j), j, s_dev).wait_send()
        share(SR2, stream_at(f * 4 + t_y, j), j, s_dev).wait_send()
        share(SR3, stream_at((1 - f) * 4 + t_y, j), j, s_dev).wait_send()
        store_copy(j).wait()


def norm_kernel(stream_ref, gain2_ref, resid_ref, normed_ref):
    t = lax.axis_index("tensor")
    squares = jnp.zeros((128, 512), jnp.float32)
    for b in range(8):
        values = stream_ref[b].reshape(128, 512).astype(jnp.float32)
        squares = squares + values * values
    scale = lax.rsqrt(jnp.sum(squares, axis=1, keepdims=True) * (1.0 / 4096.0) + epsilon)
    for b in range(8):
        part = slice(b * 512, (b + 1) * 512)
        normed_ref[0, :, part] = (
            stream_ref[b].reshape(128, 512).astype(jnp.float32) * scale * gain2_ref[:, part]
        ).astype(jnp.bfloat16)
    resid_ref[0, :, 0:512] = stream_ref[2 * t].reshape(128, 512)
    resid_ref[0, :, 512:1024] = stream_ref[2 * t + 1].reshape(128, 512)


def on_plane(
    candidates, cand_lengths, pairing, attn_gain, w_query, w_key, w_value, w_out, ffn_gain
):
    half = HEAD // 2
    inv_freq = np.float32(rope_base) ** (-np.arange(half, dtype=np.float32) * 2.0 / HEAD)
    freq = np.concatenate([inv_freq, inv_freq]).astype(np.float32)[None, :]
    angles = (np.arange(64, dtype=np.float32)[:, None] * freq).astype(np.float64)
    bf16, f32 = jnp.bfloat16, jnp.float32
    vmem = pl.BlockSpec(memory_space=pltpu.VMEM)
    hbm = pl.BlockSpec(memory_space=pl.ANY)
    stream = pl.pallas_call(
        plane_kernel,
        out_shape=jax.ShapeDtypeStruct((8, PARTS, 64, 512), bf16),
        in_specs=[pl.BlockSpec(memory_space=pltpu.SMEM)] + [vmem] * 5 + [hbm] * 5,
        out_specs=hbm,
        scratch_shapes=[
            pltpu.VMEM((16, 64, 2048), bf16),
            pltpu.VMEM((CH, 64, 1024), bf16),
            pltpu.VMEM((256, 2048), bf16),
            pltpu.VMEM((2048, 1280), bf16),
            pltpu.VMEM((1024, 2048), bf16),
            pltpu.VMEM((CH, 256, 768), bf16),
            pltpu.VMEM((CH, 256, 768), bf16),
            pltpu.VMEM((16, 64, 768), f32),
            pltpu.VMEM((CH, 8, 256), f32),
            pltpu.VMEM((CH, 8, 256), f32),
            pltpu.VMEM((8, 128), jnp.int32),
            pltpu.VMEM((16, 128), jnp.int32),
            pltpu.VMEM((PARTS, 128, 512), bf16),
            pltpu.VMEM((PARTS, 128, 512), bf16),
            pltpu.VMEM((PARTS, 128, 1024), f32),
            pltpu.VMEM((PARTS, 128, 1024), bf16),
            pltpu.VMEM((PARTS, 128, 1024), bf16),
            pltpu.VMEM((PARTS, 128, 512), bf16),
            pltpu.VMEM((PARTS, 128, 512), bf16),
            pltpu.VMEM((PARTS, 64, 512), bf16),
            pltpu.VMEM((8, PARTS, 64, 512), bf16),
            pltpu.SemaphoreType.DMA((KINDS, PARTS)),
            pltpu.SemaphoreType.DMA((KINDS, PARTS)),
            pltpu.SemaphoreType.DMA((12,)),
            pltpu.SemaphoreType.DMA((CH,)),
            pltpu.SemaphoreType.DMA((PARTS,)),
        ],
        compiler_params=pltpu.CompilerParams(
            collective_id=0, has_side_effects=True, vmem_limit_bytes=58 * 2**20
        ),
    )(
        pairing[0], cand_lengths, attn_gain.reshape(2, 1, 2048),
        jnp.asarray(np.cos(angles), f32), jnp.asarray(np.sin(angles), f32), jnp.asarray(freq),
        candidates[0], w_query, w_key, w_value, w_out,
    )
    resid, normed = pl.pallas_call(
        norm_kernel,
        grid=(CH,),
        out_shape=(
            jax.ShapeDtypeStruct((CH, 128, 1024), bf16),
            jax.ShapeDtypeStruct((CH, 128, 4096), bf16),
        ),
        in_specs=[
            pl.BlockSpec((8, 2, 64, 512), lambda k: (0, k, 0, 0)),
            pl.BlockSpec((1, 4096), lambda k: (0, 0)),
        ],
        out_specs=(
            pl.BlockSpec((1, 128, 1024), lambda k: (k, 0, 0)),
            pl.BlockSpec((1, 128, 4096), lambda k: (k, 0, 0)),
        ),
        compiler_params=pltpu.CompilerParams(vmem_limit_bytes=60 * 2**20),
    )(stream, ffn_gain.reshape(1, 4096))
    return resid[None], normed[None]


def solution(mesh):
    plane = mesh.shape["fsdp"] == 2 and mesh.shape["tensor"] == 4
    return jax.shard_map(
        on_plane if plane else on_device,
        mesh=mesh,
        in_specs=(
            P("dp", "fsdp", None, "tensor"),
            P("dp", "fsdp"),
            P("dp", None, None),
            P(),
            P("fsdp", "tensor"),
            P("fsdp", "tensor"),
            P("fsdp", "tensor"),
            P("tensor", "fsdp"),
            P(),
        ),
        out_specs=(P("dp", "fsdp", None, "tensor"), P("dp", "fsdp", None, None)),
        check_vma=False,
    )
```

```python
import jax
import jax.numpy as jnp
import numpy as np
from jax import lax
from jax.experimental import pallas as pl
from jax.experimental.pallas import tpu as pltpu
from jax.sharding import PartitionSpec as P

HEAD = 128


epsilon = 1e-05
rope_base = 500000.0


def rms_scale(values, gain):
    mean_square = jnp.mean(values * values, axis=-1, keepdims=True)
    return values * lax.rsqrt(mean_square + epsilon) * gain


def positions_of(lengths, sample):
    slot_steps = jnp.arange(2 * sample, dtype=jnp.int32)
    return jnp.where(slot_steps < sample, slot_steps, lengths[..., :1] + slot_steps - sample)


def key_mask(lengths, sample):
    slot_steps = jnp.arange(2 * sample, dtype=jnp.int32)
    local_step = jnp.where(slot_steps < sample, slot_steps, slot_steps - sample)
    limit = jnp.where(slot_steps < sample, lengths[..., :1], lengths[..., 1:])
    valid = local_step < limit
    causal = slot_steps[None, :] <= slot_steps[:, None]
    return causal[None] & valid[:, None, :]


def rotate(values, positions, head_size):
    half = head_size // 2
    inv_freq = rope_base ** (-jnp.arange(half, dtype=jnp.float32) * 2.0 / head_size)
    angles = positions.astype(jnp.float32)[..., None] * inv_freq
    cosine = jnp.cos(angles)[..., None, :]
    sine_table = jnp.sin(angles)[..., None, :]
    lower = values[..., :half]
    upper = values[..., half:]
    return jnp.concatenate(
        [lower * cosine - upper * sine_table, upper * cosine + lower * sine_table], axis=-1
    )


def attend(query, key_rows, value_rows, allowed):
    pair_rows, row_count, kv_count, group_size, head_size = query.shape
    scores = jnp.einsum(
        "bqkgd,bskd->bkgqs", query, key_rows, preferred_element_type=jnp.float32
    ) * head_size ** (-0.5)
    scores = jnp.where(allowed[:, None, None], scores, -1e30)
    row_peak = jnp.max(scores, axis=-1, keepdims=True)
    weights = jnp.exp(scores - row_peak)
    prob_rows = (weights / jnp.sum(weights, axis=-1, keepdims=True)).astype(jnp.bfloat16)
    mixed_rows = jnp.einsum(
        "bkgqs,bskd->bqkgd", prob_rows, value_rows, preferred_element_type=jnp.float32
    )
    return mixed_rows.astype(jnp.bfloat16).reshape(
        pair_rows * row_count, kv_count * group_size * head_size
    )


def on_device(
    candidates, cand_lengths, pairing, attn_gain, w_query, w_key, w_value, w_out, ffn_gain
):
    fsdp_count = lax.axis_size("fsdp")
    my_index = lax.axis_index("fsdp")
    cand_dev = candidates.shape[1]
    sample = candidates.shape[2]
    share_width = candidates.shape[3]
    pair_dev = cand_dev // 2
    most_slots = max(1, cand_dev // fsdp_count)
    flat_slots = pairing[0].reshape(-1)
    slot_count = flat_slots.shape[0]
    every_slot = jnp.arange(slot_count, dtype=jnp.int32)
    matches = flat_slots[:, None] == every_slot[None, :]
    target_slot = jnp.sum(jnp.where(matches, every_slot[:, None], 0), axis=0)
    target_dev = target_slot // cand_dev
    source_dev = every_slot // cand_dev
    earlier = (
        (source_dev[:, None] == source_dev[None, :])
        & (target_dev[:, None] == target_dev[None, :])
        & (every_slot[None, :] < every_slot[:, None])
    )
    send_rank = jnp.sum(earlier.astype(jnp.int32), axis=1)
    place = target_dev * most_slots + send_rank
    arrive = source_dev * most_slots + send_rank
    own_cands = my_index * cand_dev + jnp.arange(cand_dev, dtype=jnp.int32)
    own_pick = own_cands[:, None] == every_slot[None, :]
    own_place = jnp.sum(jnp.where(own_pick, place[None, :], 0), axis=1)
    buffer_slots = jnp.arange(fsdp_count * most_slots, dtype=jnp.int32)
    sender = buffer_slots[:, None] == own_place[None, :]
    outgoing = jnp.einsum(
        "bc,csf->bsf",
        sender.astype(jnp.bfloat16),
        candidates[0],
        preferred_element_type=jnp.float32,
    ).astype(jnp.bfloat16)
    out_lengths = jnp.sum(jnp.where(sender, cand_lengths[0][None, :], 0), axis=1)
    incoming, in_lengths = (
        lax.all_to_all(
            outgoing.reshape(fsdp_count, most_slots, sample, share_width),
            "fsdp",
            split_axis=0,
            concat_axis=0,
            tiled=True,
        ),
        lax.all_to_all(
            out_lengths.reshape(fsdp_count, most_slots),
            "fsdp",
            split_axis=0,
            concat_axis=0,
            tiled=True,
        ),
    )
    slot_pick = own_cands[:, None] == every_slot[None, :]
    wanted = jnp.sum(jnp.where(slot_pick, flat_slots[None, :], 0), axis=1)
    wanted_pick = wanted[:, None] == every_slot[None, :]
    wanted_from = jnp.sum(jnp.where(wanted_pick, arrive[None, :], 0), axis=1)
    receiver = wanted_from[:, None] == buffer_slots[None, :]
    local_rows = jnp.einsum(
        "cb,bsf->csf",
        receiver.astype(jnp.bfloat16),
        incoming.reshape(-1, sample, share_width),
        preferred_element_type=jnp.float32,
    ).astype(jnp.bfloat16)
    row_lengths = (
        jnp.sum(jnp.where(receiver, in_lengths.reshape(-1)[None, :], 0), axis=1)
        .astype(jnp.int32)
        .reshape(pair_dev, 2)
    )
    full_rows = lax.all_gather(local_rows, "tensor", axis=2, tiled=True)
    width = full_rows.shape[2]
    tok_count = cand_dev * sample
    inputs = full_rows.reshape(tok_count, width).astype(jnp.float32)
    normal_rows = rms_scale(inputs, attn_gain).astype(jnp.bfloat16)
    query_cols = w_query.shape[1]
    key_cols = w_key.shape[1]
    query = jnp.dot(
        normal_rows,
        lax.all_gather(w_query, "fsdp", axis=0, tiled=True),
        preferred_element_type=jnp.float32,
    )
    key_rows = jnp.dot(
        normal_rows,
        lax.all_gather(w_key, "fsdp", axis=0, tiled=True),
        preferred_element_type=jnp.float32,
    )
    value_rows = jnp.dot(
        normal_rows,
        lax.all_gather(w_value, "fsdp", axis=0, tiled=True),
        preferred_element_type=jnp.float32,
    )
    heads_here = query_cols // HEAD
    kv_here = key_cols // HEAD
    positions = positions_of(row_lengths, sample)
    query = rotate(query.reshape(pair_dev, 2 * sample, heads_here, HEAD), positions, HEAD).astype(
        jnp.bfloat16
    )
    key_rows = rotate(
        key_rows.reshape(pair_dev, 2 * sample, kv_here, HEAD), positions, HEAD
    ).astype(jnp.bfloat16)
    value_rows = value_rows.astype(jnp.bfloat16).reshape(pair_dev, 2 * sample, kv_here, HEAD)
    query = query.reshape(pair_dev, 2 * sample, kv_here, heads_here // kv_here, HEAD)
    mixed = attend(query, key_rows, value_rows, key_mask(row_lengths, sample))
    branch = jnp.dot(
        mixed, lax.all_gather(w_out, "fsdp", axis=1, tiled=True), preferred_element_type=jnp.float32
    )
    tensor_offset = lax.axis_index("tensor") * share_width
    summed_branch = lax.psum(branch.astype(jnp.bfloat16), "tensor").astype(jnp.float32)
    stream = inputs + summed_branch
    normed = rms_scale(stream, ffn_gain).astype(jnp.bfloat16)
    resid = lax.dynamic_slice_in_dim(stream, tensor_offset, share_width, 1).astype(jnp.bfloat16)
    return (
        resid.reshape(1, pair_dev, 2 * sample, share_width),
        normed.reshape(1, pair_dev, 2 * sample, width),
    )


MESH = pl.DeviceIdType.MESH
CH = 8
PARTS = 8
X1, Y1, Y2, S1A, S1B, S1C, XQ, XS, XM, SB, YB, XR, YR1, YR2, SR0, SR1, SR2, SR3, LN = range(19)
KINDS = 19


def plane_kernel(
    pair_ref, lens_ref, gain1_ref, cos_ref, sin_ref, freq_ref,
    cand_ref, wq_ref, wk_ref, wv_ref, wo_ref,
    stream_ref,
    grid_x, relay, lhs, w_in, w_out, q_send, q_recv, q_own, ss_own, ss_recv, own_lens, lens_all,
    mix_own, mix_recv, acc_own, sib_send, sib_recv, y_send, y_recv, x_send, stream,
    send_sem, recv_sem, load_sem, local_sem, store_sem,
):
    f = lax.axis_index("fsdp")
    t = lax.axis_index("tensor")
    y = t // 2
    c = t % 2
    x_dev = {"fsdp": 1 - f}
    t_y = (t + 2) % 4
    t_s = t + 1 - 2 * c
    t_sy = (t_s + 2) % 4
    y_dev = {"tensor": t_y}
    s_dev = {"tensor": t_s}
    even = f == y

    def remote(kind, j, src, dst, dev):
        return pltpu.make_async_remote_copy(
            src_ref=src, dst_ref=dst, send_sem=send_sem.at[kind, j],
            recv_sem=recv_sem.at[kind, j], device_id=dev, device_id_type=MESH,
        )

    loads = []

    def load(src, dst):
        copy = pltpu.make_async_copy(src, dst, load_sem.at[len(loads)])
        copy.start()
        loads.append(copy)

    mine = pl.multiple_of(f * 512, 512)
    other = pl.multiple_of((1 - f) * 512, 512)
    load(wq_ref.at[:, pl.ds(mine, 512)], w_in.at[:, 0:512])
    load(wq_ref.at[:, pl.ds(other, 512)], w_in.at[:, 512:1024])
    load(wk_ref, w_in.at[:, 1024:1152])
    load(wv_ref, w_in.at[:, 1152:1280])
    for r, row in enumerate((mine, other)):
        for b, block in enumerate((t, t_y, t_s, t_sy)):
            load(
                wo_ref.at[pl.ds(row, 512), pl.ds(pl.multiple_of(block * 512, 512), 512)],
                w_out.at[r * 512:(r + 1) * 512, b * 512:(b + 1) * 512],
            )

    barrier = pltpu.get_barrier_semaphore()
    for dev in (x_dev, y_dev, s_dev):
        pl.semaphore_signal(barrier, inc=1, device_id=dev, device_id_type=MESH)
    pl.semaphore_wait(barrier, 3)

    spread = jnp.broadcast_to(lens_ref[...].astype(jnp.float32), (8, 8))
    pick = lax.broadcasted_iota(jnp.int32, (8, 8), 0) == lax.broadcasted_iota(jnp.int32, (8, 8), 1)
    column = jnp.sum(jnp.where(pick, spread, 0.0), axis=1, keepdims=True)
    own_lens[...] = jnp.broadcast_to(column, (8, 128)).astype(jnp.int32)
    lens_copy = remote(LN, 0, own_lens, lens_all.at[pl.ds(pl.multiple_of(f * 8, 8), 8)], x_dev)
    lens_copy.start()
    lens_all[pl.ds(pl.multiple_of(f * 8, 8), 8), :] = own_lens[...]

    cols = pl.ds(pl.multiple_of(c * 1024, 1024), 1024)

    def place(g, j, at=0, count=2):
        return grid_x.at[pl.ds(g * 8 + j, 1), at * 32:(at + count) * 32, cols]

    def own(j, at=0, count=2):
        return cand_ref.at[j:j + 1, at * 32:(at + count) * 32]

    def hop(j):
        return relay.at[j:j + 1]

    def local_copy(j):
        return pltpu.make_async_copy(own(j), place(f, j), local_sem.at[j])

    def send_y(j):
        @pl.when(even)
        def _():
            remote(Y1, j, own(j), place(f, j), y_dev).start()

        @pl.when(jnp.logical_not(even))
        def _():
            remote(Y1, j, own(j, 1, 1), hop(j), y_dev).start()

    def far_x(j, at):
        return place(1 - f, j, at, 1)

    def forward_x(j):
        @pl.when(even)
        def _():
            remote(Y1, j, own(j, 1, 1), hop(j), y_dev).wait_recv()
            remote(X1, j, hop(j), place(f, j, 1, 1), x_dev).start()

    def forward_y(j):
        @pl.when(even)
        def _():
            remote(X1, j, own(j, 0, 1), far_x(j, 0), x_dev).wait_recv()
            remote(Y2, j, far_x(j, 0), far_x(j, 0), y_dev).start()
            remote(S1B, j, far_x(j, 0), far_x(j, 0), s_dev).start()
            local_copy(j).wait()

        @pl.when(jnp.logical_not(even))
        def _():
            remote(X1, j, hop(j), far_x(j, 1), x_dev).wait_recv()
            remote(Y2, j, far_x(j, 1), far_x(j, 1), y_dev).start()
            remote(S1B, j, far_x(j, 1), far_x(j, 1), s_dev).start()
            remote(Y1, j, own(j), place(f, j), y_dev).wait_recv()

        remote(S1A, j, place(f, j), place(f, j), s_dev).start()

    def finish_input(j):
        def last(at):
            remote(Y2, j, far_x(j, at), far_x(j, at), y_dev).wait_recv()
            remote(S1C, j, far_x(j, at), far_x(j, at), s_dev).start()
            remote(S1B, j, far_x(j, 1 - at), far_x(j, 1 - at), s_dev).wait_recv()
            remote(S1C, j, far_x(j, at), far_x(j, at), s_dev).wait_recv()

        @pl.when(even)
        def _():
            last(1)

        @pl.when(jnp.logical_not(even))
        def _():
            last(0)

        remote(S1A, j, place(f, j), place(f, j), s_dev).wait_recv()

    def send_x(j):
        @pl.when(jnp.logical_not(even))
        def _():
            remote(X1, j, own(j, 0, 1), place(f, j, 0, 1), x_dev).start()

    for j in range(2):
        send_y(j)
        send_x(j)

    @pl.when(even)
    def _():
        for j in range(CH):
            local_copy(j).start()

    for copy in loads[:4]:
        copy.wait()

    def finish(j):
        remote(XQ, j, q_send.at[j], q_recv.at[j], x_dev).wait_recv()
        remote(XS, j, ss_own.at[j], ss_recv.at[j], x_dev).wait_recv()
        total = (ss_own[j] + ss_recv[j])[0:1, :]
        scale = lax.rsqrt(total * (1.0 / 4096.0) + epsilon)
        column = jnp.broadcast_to(scale, (128, 128)).T
        for m in range(6):
            part = slice(m * 128, (m + 1) * 128)
            summed = q_own[2 * j:2 * j + 2, :, part].reshape(128, 128) + q_recv[
                j, :, part
            ].astype(jnp.float32)
            q_own[2 * j:2 * j + 2, :, part] = (summed * column).reshape(2, 64, 128)

    forward_x(0)
    for j in range(CH):
        forward_y(j)
        if j + 1 < CH:
            forward_x(j + 1)
        if j + 2 < CH:
            send_y(j + 2)
            send_x(j + 2)
        finish_input(j)

        gain = gain1_ref[f]
        squares = []
        for g in range(2):
            values = grid_x[g * 8 + j].astype(jnp.float32)
            squares.append(jnp.sum(values * values, axis=1, keepdims=True))
            lhs[g * 64:(g + 1) * 64, :] = (values * gain).astype(jnp.bfloat16)
        ss_own[j] = jnp.broadcast_to(jnp.concatenate(squares, axis=0), (128, 128)).T[0:8]

        def project(n):
            return jnp.dot(
                lhs[...],
                w_in[:, pl.ds(pl.multiple_of(n * 256, 256), 256)],
                preferred_element_type=jnp.float32,
            )

        @pl.loop(0, 3)
        def _(n):
            result = project(n + 2)
            at = pl.ds(pl.multiple_of(n * 256, 256), 256)
            q_send[j, :, at] = result.astype(jnp.bfloat16)

        q_own[2 * j:2 * j + 2, :, 512:768] = project(4).reshape(2, 64, 256)
        remote(XQ, j, q_send.at[j], q_recv.at[j], x_dev).start()
        remote(XS, j, ss_own.at[j], ss_recv.at[j], x_dev).start()

        @pl.loop(0, 2)
        def _(n):
            result = project(n)
            at = pl.ds(pl.multiple_of(n * 256, 256), 256)
            q_own[2 * j:2 * j + 2, :, at] = result.reshape(2, 64, 256)

        if j > 2:
            finish(j - 3)
    for j in range(CH - 3, CH):
        finish(j)
    lens_copy.wait()

    lane = lax.broadcasted_iota(jnp.int32, (1, 128), 1)
    sign = jnp.where(lane < 64, -1.0, 1.0)
    slot_t = lax.broadcasted_iota(jnp.int32, (128, 128), 0)
    slot_u = lax.broadcasted_iota(jnp.int32, (128, 128), 1)

    def packed(cand):
        return (cand % 8) * 2 + cand // 8

    def attention(k, half):
        row = half * 4 + k
        cand0, cand1 = pair_ref[row, 0], pair_ref[row, 1]
        at0, at1 = packed(cand0), packed(cand1)
        len0 = lens_all[pl.ds(cand0, 1), :]
        len1 = lens_all[pl.ds(cand1, 1), :]
        angle = len0.astype(jnp.float32) * freq_ref[...]
        shift_cos, shift_sin = jnp.cos(angle), jnp.sin(angle)
        cos0, sin0 = cos_ref[...], sin_ref[...]
        cosine = jnp.concatenate([cos0, cos0 * shift_cos - sin0 * shift_sin], axis=0)
        sine = jnp.concatenate([sin0, sin0 * shift_cos + cos0 * shift_sin], axis=0) * sign
        allowed = (slot_u <= slot_t) & (lane < jnp.where(lane < 64, len0, len1 + 64))

        def block(m):
            part = slice(m * 128, (m + 1) * 128)
            return jnp.concatenate([q_own[at0, :, part], q_own[at1, :, part]], axis=0)

        def turned(m):
            values = block(m)
            return (values * cosine + pltpu.roll(values, 64, axis=1) * sine).astype(jnp.bfloat16)

        keys = turned(4)
        value_rows = block(5).astype(jnp.bfloat16)
        queries = jnp.concatenate([turned(h) for h in range(4)], axis=0)
        scores = lax.dot_general(
            queries, keys, (((1,), (1,)), ((), ())), preferred_element_type=jnp.float32
        ) * HEAD ** (-0.5)
        scores = jnp.where(jnp.concatenate([allowed] * 4, axis=0), scores, -1e30)
        weights = jnp.exp(scores - jnp.max(scores, axis=1, keepdims=True))
        probs = weights * (1.0 / jnp.sum(weights, axis=1, keepdims=True))
        mixed = jnp.dot(
            probs.astype(jnp.bfloat16), value_rows, preferred_element_type=jnp.float32
        ).astype(jnp.bfloat16)
        for h in range(4):
            for s in range(2):
                mix_own[2 * k + s, half * 64:(half + 1) * 64, h * 128:(h + 1) * 128] = mixed[
                    h * 128 + s * 64:h * 128 + (s + 1) * 64
                ]

    def stream_at(block, k):
        return stream.at[block, k]

    def own_block(k):
        return stream_at(f * 4 + t, k)

    def far_block(k):
        return stream_at((1 - f) * 4 + t, k)

    def share(kind, ref, k, dev):
        return remote(kind, k, ref, ref, dev)

    def mix_copy(k):
        return remote(XM, k, mix_own.at[k], mix_recv.at[k], x_dev)

    def partial_copy(k):
        return remote(SB, k, sib_send.at[k], sib_recv.at[k], s_dev)

    def pair_copy(k):
        return remote(YB, k, y_send.at[k], y_recv.at[k], y_dev)

    def cross_copy(k):
        return remote(XR, k, x_send.at[k], own_block(k), x_dev)

    def project_out(k):
        mix_copy(k).wait_recv()

        def term(n):
            at = pl.ds(pl.multiple_of(n * 256, 256), 256)
            return jnp.dot(
                mix_own[k], w_out[0:512, at], preferred_element_type=jnp.float32
            ) + jnp.dot(mix_recv[k], w_out[512:1024, at], preferred_element_type=jnp.float32)

        @pl.loop(0, 4)
        def _(n):
            at = pl.ds(pl.multiple_of(n * 256, 256), 256)
            sib_send[k, :, at] = term(n + 4).astype(jnp.bfloat16)

        partial_copy(k).start()

        @pl.loop(0, 4)
        def _(n):
            acc_own[k, :, pl.ds(pl.multiple_of(n * 256, 256), 256)] = term(n)

    def add_sibling(k):
        partial_copy(k).wait_recv()
        y_send[k] = (acc_own[k, :, 512:] + sib_recv[k, :, 512:].astype(jnp.float32)).astype(
            jnp.bfloat16
        )
        pair_copy(k).start()
        acc_own[k, :, 0:512] = acc_own[k, :, 0:512] + sib_recv[k, :, 0:512].astype(jnp.float32)

    def add_rows(k):
        pair_copy(k).wait_recv()
        at = pl.ds(pl.multiple_of(t * 512, 512), 512)
        parts = []
        for half in range(2):
            rows = grid_x[pair_ref[half * 4 + k // 2, k % 2], :, at]
            part = slice(half * 64, (half + 1) * 64)
            branch = acc_own[k, part, 0:512] + y_recv[k, part, :].astype(jnp.float32)
            parts.append(rows.astype(jnp.float32) + branch)
        first = f == 0
        x_send[k] = jnp.where(first, parts[1], parts[0]).astype(jnp.bfloat16)
        cross_copy(k).start()
        stream[f * 4 + t, k] = jnp.where(first, parts[0], parts[1]).astype(jnp.bfloat16)
        share(YR1, own_block(k), k, y_dev).start()
        share(SR0, own_block(k), k, s_dev).start()

    def pass_far(k):
        remote(XR, k, x_send.at[k], far_block(k), x_dev).wait_recv()
        share(YR2, far_block(k), k, y_dev).start()
        share(SR1, far_block(k), k, s_dev).start()

    def pass_pair(k):
        near = stream_at(f * 4 + t_y, k)
        far = stream_at((1 - f) * 4 + t_y, k)
        share(YR1, near, k, y_dev).wait_recv()
        share(SR2, near, k, s_dev).start()
        share(YR2, far, k, y_dev).wait_recv()
        share(SR3, far, k, s_dev).start()

    def store_copy(k):
        return pltpu.make_async_copy(stream.at[:, k], stream_ref.at[:, k], store_sem.at[k])

    def store(k):
        share(SR0, stream_at(f * 4 + t_s, k), k, s_dev).wait_recv()
        share(SR1, stream_at((1 - f) * 4 + t_s, k), k, s_dev).wait_recv()
        share(SR2, stream_at(f * 4 + t_sy, k), k, s_dev).wait_recv()
        share(SR3, stream_at((1 - f) * 4 + t_sy, k), k, s_dev).wait_recv()
        store_copy(k).start()

    for copy in loads[4:]:
        copy.wait()
    def attend_rows(k):
        attention(k, 0)
        attention(k, 1)
        mix_copy(2 * k).start()
        mix_copy(2 * k + 1).start()

    order = [(2.0 * j - 2.5, attend_rows, j) for j in range(PARTS // 2)]
    for lag, stage in (
        (0.0, project_out), (0.8, add_sibling), (2.1, add_rows),
        (3.2, pass_far), (4.3, pass_pair), (5.4, store),
    ):
        order += [(k + lag, stage, k) for k in range(PARTS)]
    for _, stage, k in sorted(order, key=lambda item: item[0]):
        stage(k)

    for j in range(CH):

        @pl.when(even)
        def _():
            remote(Y1, j, own(j), place(f, j), y_dev).wait_send()
            remote(X1, j, hop(j), place(f, j, 1, 1), x_dev).wait_send()
            remote(Y2, j, far_x(j, 0), far_x(j, 0), y_dev).wait_send()
            remote(S1B, j, far_x(j, 0), far_x(j, 0), s_dev).wait_send()
            remote(S1C, j, far_x(j, 1), far_x(j, 1), s_dev).wait_send()

        @pl.when(jnp.logical_not(even))
        def _():
            remote(Y1, j, own(j, 1, 1), hop(j), y_dev).wait_send()
            remote(X1, j, own(j, 0, 1), place(f, j, 0, 1), x_dev).wait_send()
            remote(Y2, j, far_x(j, 1), far_x(j, 1), y_dev).wait_send()
            remote(S1B, j, far_x(j, 1), far_x(j, 1), s_dev).wait_send()
            remote(S1C, j, far_x(j, 0), far_x(j, 0), s_dev).wait_send()

        remote(S1A, j, place(f, j), place(f, j), s_dev).wait_send()
        remote(XQ, j, q_send.at[j], q_recv.at[j], x_dev).wait_send()
        remote(XS, j, ss_own.at[j], ss_recv.at[j], x_dev).wait_send()
    for j in range(PARTS):
        mix_copy(j).wait_send()
        partial_copy(j).wait_send()
        pair_copy(j).wait_send()
        cross_copy(j).wait_send()
        share(YR1, own_block(j), j, y_dev).wait_send()
        share(SR0, own_block(j), j, s_dev).wait_send()
        share(YR2, far_block(j), j, y_dev).wait_send()
        share(SR1, far_block(j), j, s_dev).wait_send()
        share(SR2, stream_at(f * 4 + t_y, j), j, s_dev).wait_send()
        share(SR3, stream_at((1 - f) * 4 + t_y, j), j, s_dev).wait_send()
        store_copy(j).wait()


def norm_kernel(stream_ref, gain2_ref, resid_ref, normed_ref):
    t = lax.axis_index("tensor")
    squares = jnp.zeros((128, 512), jnp.float32)
    for b in range(8):
        values = stream_ref[b].reshape(128, 512).astype(jnp.float32)
        squares = squares + values * values
    scale = lax.rsqrt(jnp.sum(squares, axis=1, keepdims=True) * (1.0 / 4096.0) + epsilon)
    for b in range(8):
        part = slice(b * 512, (b + 1) * 512)
        normed_ref[0, :, part] = (
            stream_ref[b].reshape(128, 512).astype(jnp.float32) * scale * gain2_ref[:, part]
        ).astype(jnp.bfloat16)
    resid_ref[0, :, 0:512] = stream_ref[2 * t].reshape(128, 512)
    resid_ref[0, :, 512:1024] = stream_ref[2 * t + 1].reshape(128, 512)


def on_plane(
    candidates, cand_lengths, pairing, attn_gain, w_query, w_key, w_value, w_out, ffn_gain
):
    half = HEAD // 2
    inv_freq = np.float32(rope_base) ** (-np.arange(half, dtype=np.float32) * 2.0 / HEAD)
    freq = np.concatenate([inv_freq, inv_freq]).astype(np.float32)[None, :]
    angles = (np.arange(64, dtype=np.float32)[:, None] * freq).astype(np.float64)
    bf16, f32 = jnp.bfloat16, jnp.float32
    vmem = pl.BlockSpec(memory_space=pltpu.VMEM)
    hbm = pl.BlockSpec(memory_space=pl.ANY)
    stream = pl.pallas_call(
        plane_kernel,
        out_shape=jax.ShapeDtypeStruct((8, PARTS, 64, 512), bf16),
        in_specs=[pl.BlockSpec(memory_space=pltpu.SMEM)] + [vmem] * 5 + [hbm] * 5,
        out_specs=hbm,
        scratch_shapes=[
            pltpu.VMEM((16, 64, 2048), bf16),
            pltpu.VMEM((CH, 32, 1024), bf16),
            pltpu.VMEM((128, 2048), bf16),
            pltpu.VMEM((2048, 1280), bf16),
            pltpu.VMEM((1024, 2048), bf16),
            pltpu.VMEM((CH, 128, 768), bf16),
            pltpu.VMEM((CH, 128, 768), bf16),
            pltpu.VMEM((16, 64, 768), f32),
            pltpu.VMEM((CH, 8, 128), f32),
            pltpu.VMEM((CH, 8, 128), f32),
            pltpu.VMEM((8, 128), jnp.int32),
            pltpu.VMEM((16, 128), jnp.int32),
            pltpu.VMEM((PARTS, 128, 512), bf16),
            pltpu.VMEM((PARTS, 128, 512), bf16),
            pltpu.VMEM((PARTS, 128, 1024), f32),
            pltpu.VMEM((PARTS, 128, 1024), bf16),
            pltpu.VMEM((PARTS, 128, 1024), bf16),
            pltpu.VMEM((PARTS, 128, 512), bf16),
            pltpu.VMEM((PARTS, 128, 512), bf16),
            pltpu.VMEM((PARTS, 64, 512), bf16),
            pltpu.VMEM((8, PARTS, 64, 512), bf16),
            pltpu.SemaphoreType.DMA((KINDS, PARTS)),
            pltpu.SemaphoreType.DMA((KINDS, PARTS)),
            pltpu.SemaphoreType.DMA((12,)),
            pltpu.SemaphoreType.DMA((CH,)),
            pltpu.SemaphoreType.DMA((PARTS,)),
        ],
        compiler_params=pltpu.CompilerParams(
            collective_id=0, has_side_effects=True, vmem_limit_bytes=58 * 2**20
        ),
    )(
        pairing[0], cand_lengths, attn_gain.reshape(2, 1, 2048),
        jnp.asarray(np.cos(angles), f32), jnp.asarray(np.sin(angles), f32), jnp.asarray(freq),
        candidates[0], w_query, w_key, w_value, w_out,
    )
    resid, normed = pl.pallas_call(
        norm_kernel,
        grid=(PARTS // 2,),
        out_shape=(
            jax.ShapeDtypeStruct((PARTS // 2, 128, 1024), bf16),
            jax.ShapeDtypeStruct((PARTS // 2, 128, 4096), bf16),
        ),
        in_specs=[
            pl.BlockSpec((8, 2, 64, 512), lambda k: (0, k, 0, 0)),
            pl.BlockSpec((1, 4096), lambda k: (0, 0)),
        ],
        out_specs=(
            pl.BlockSpec((1, 128, 1024), lambda k: (k, 0, 0)),
            pl.BlockSpec((1, 128, 4096), lambda k: (k, 0, 0)),
        ),
        compiler_params=pltpu.CompilerParams(vmem_limit_bytes=60 * 2**20),
    )(stream, ffn_gain.reshape(1, 4096))
    return resid[None], normed[None]


def solution(mesh):
    plane = mesh.shape["fsdp"] == 2 and mesh.shape["tensor"] == 4
    return jax.shard_map(
        on_plane if plane else on_device,
        mesh=mesh,
        in_specs=(
            P("dp", "fsdp", None, "tensor"),
            P("dp", "fsdp"),
            P("dp", None, None),
            P(),
            P("fsdp", "tensor"),
            P("fsdp", "tensor"),
            P("fsdp", "tensor"),
            P("tensor", "fsdp"),
            P(),
        ),
        out_specs=(P("dp", "fsdp", None, "tensor"), P("dp", "fsdp", None, None)),
        check_vma=False,
    )
```

```python
import jax
import jax.numpy as jnp
import numpy as np
from jax import lax
from jax.experimental import pallas as pl
from jax.experimental.pallas import tpu as pltpu
from jax.sharding import PartitionSpec as P

HEAD = 128


epsilon = 1e-05
rope_base = 500000.0


def rms_scale(values, gain):
    mean_square = jnp.mean(values * values, axis=-1, keepdims=True)
    return values * lax.rsqrt(mean_square + epsilon) * gain


def positions_of(lengths, sample):
    slot_steps = jnp.arange(2 * sample, dtype=jnp.int32)
    return jnp.where(slot_steps < sample, slot_steps, lengths[..., :1] + slot_steps - sample)


def key_mask(lengths, sample):
    slot_steps = jnp.arange(2 * sample, dtype=jnp.int32)
    local_step = jnp.where(slot_steps < sample, slot_steps, slot_steps - sample)
    limit = jnp.where(slot_steps < sample, lengths[..., :1], lengths[..., 1:])
    valid = local_step < limit
    causal = slot_steps[None, :] <= slot_steps[:, None]
    return causal[None] & valid[:, None, :]


def rotate(values, positions, head_size):
    half = head_size // 2
    inv_freq = rope_base ** (-jnp.arange(half, dtype=jnp.float32) * 2.0 / head_size)
    angles = positions.astype(jnp.float32)[..., None] * inv_freq
    cosine = jnp.cos(angles)[..., None, :]
    sine_table = jnp.sin(angles)[..., None, :]
    lower = values[..., :half]
    upper = values[..., half:]
    return jnp.concatenate(
        [lower * cosine - upper * sine_table, upper * cosine + lower * sine_table], axis=-1
    )


def attend(query, key_rows, value_rows, allowed):
    pair_rows, row_count, kv_count, group_size, head_size = query.shape
    scores = jnp.einsum(
        "bqkgd,bskd->bkgqs", query, key_rows, preferred_element_type=jnp.float32
    ) * head_size ** (-0.5)
    scores = jnp.where(allowed[:, None, None], scores, -1e30)
    row_peak = jnp.max(scores, axis=-1, keepdims=True)
    weights = jnp.exp(scores - row_peak)
    prob_rows = (weights / jnp.sum(weights, axis=-1, keepdims=True)).astype(jnp.bfloat16)
    mixed_rows = jnp.einsum(
        "bkgqs,bskd->bqkgd", prob_rows, value_rows, preferred_element_type=jnp.float32
    )
    return mixed_rows.astype(jnp.bfloat16).reshape(
        pair_rows * row_count, kv_count * group_size * head_size
    )


def on_device(
    candidates, cand_lengths, pairing, attn_gain, w_query, w_key, w_value, w_out, ffn_gain
):
    fsdp_count = lax.axis_size("fsdp")
    my_index = lax.axis_index("fsdp")
    cand_dev = candidates.shape[1]
    sample = candidates.shape[2]
    share_width = candidates.shape[3]
    pair_dev = cand_dev // 2
    most_slots = max(1, cand_dev // fsdp_count)
    flat_slots = pairing[0].reshape(-1)
    slot_count = flat_slots.shape[0]
    every_slot = jnp.arange(slot_count, dtype=jnp.int32)
    matches = flat_slots[:, None] == every_slot[None, :]
    target_slot = jnp.sum(jnp.where(matches, every_slot[:, None], 0), axis=0)
    target_dev = target_slot // cand_dev
    source_dev = every_slot // cand_dev
    earlier = (
        (source_dev[:, None] == source_dev[None, :])
        & (target_dev[:, None] == target_dev[None, :])
        & (every_slot[None, :] < every_slot[:, None])
    )
    send_rank = jnp.sum(earlier.astype(jnp.int32), axis=1)
    place = target_dev * most_slots + send_rank
    arrive = source_dev * most_slots + send_rank
    own_cands = my_index * cand_dev + jnp.arange(cand_dev, dtype=jnp.int32)
    own_pick = own_cands[:, None] == every_slot[None, :]
    own_place = jnp.sum(jnp.where(own_pick, place[None, :], 0), axis=1)
    buffer_slots = jnp.arange(fsdp_count * most_slots, dtype=jnp.int32)
    sender = buffer_slots[:, None] == own_place[None, :]
    outgoing = jnp.einsum(
        "bc,csf->bsf",
        sender.astype(jnp.bfloat16),
        candidates[0],
        preferred_element_type=jnp.float32,
    ).astype(jnp.bfloat16)
    out_lengths = jnp.sum(jnp.where(sender, cand_lengths[0][None, :], 0), axis=1)
    incoming, in_lengths = (
        lax.all_to_all(
            outgoing.reshape(fsdp_count, most_slots, sample, share_width),
            "fsdp",
            split_axis=0,
            concat_axis=0,
            tiled=True,
        ),
        lax.all_to_all(
            out_lengths.reshape(fsdp_count, most_slots),
            "fsdp",
            split_axis=0,
            concat_axis=0,
            tiled=True,
        ),
    )
    slot_pick = own_cands[:, None] == every_slot[None, :]
    wanted = jnp.sum(jnp.where(slot_pick, flat_slots[None, :], 0), axis=1)
    wanted_pick = wanted[:, None] == every_slot[None, :]
    wanted_from = jnp.sum(jnp.where(wanted_pick, arrive[None, :], 0), axis=1)
    receiver = wanted_from[:, None] == buffer_slots[None, :]
    local_rows = jnp.einsum(
        "cb,bsf->csf",
        receiver.astype(jnp.bfloat16),
        incoming.reshape(-1, sample, share_width),
        preferred_element_type=jnp.float32,
    ).astype(jnp.bfloat16)
    row_lengths = (
        jnp.sum(jnp.where(receiver, in_lengths.reshape(-1)[None, :], 0), axis=1)
        .astype(jnp.int32)
        .reshape(pair_dev, 2)
    )
    full_rows = lax.all_gather(local_rows, "tensor", axis=2, tiled=True)
    width = full_rows.shape[2]
    tok_count = cand_dev * sample
    inputs = full_rows.reshape(tok_count, width).astype(jnp.float32)
    normal_rows = rms_scale(inputs, attn_gain).astype(jnp.bfloat16)
    query_cols = w_query.shape[1]
    key_cols = w_key.shape[1]
    query = jnp.dot(
        normal_rows,
        lax.all_gather(w_query, "fsdp", axis=0, tiled=True),
        preferred_element_type=jnp.float32,
    )
    key_rows = jnp.dot(
        normal_rows,
        lax.all_gather(w_key, "fsdp", axis=0, tiled=True),
        preferred_element_type=jnp.float32,
    )
    value_rows = jnp.dot(
        normal_rows,
        lax.all_gather(w_value, "fsdp", axis=0, tiled=True),
        preferred_element_type=jnp.float32,
    )
    heads_here = query_cols // HEAD
    kv_here = key_cols // HEAD
    positions = positions_of(row_lengths, sample)
    query = rotate(query.reshape(pair_dev, 2 * sample, heads_here, HEAD), positions, HEAD).astype(
        jnp.bfloat16
    )
    key_rows = rotate(
        key_rows.reshape(pair_dev, 2 * sample, kv_here, HEAD), positions, HEAD
    ).astype(jnp.bfloat16)
    value_rows = value_rows.astype(jnp.bfloat16).reshape(pair_dev, 2 * sample, kv_here, HEAD)
    query = query.reshape(pair_dev, 2 * sample, kv_here, heads_here // kv_here, HEAD)
    mixed = attend(query, key_rows, value_rows, key_mask(row_lengths, sample))
    branch = jnp.dot(
        mixed, lax.all_gather(w_out, "fsdp", axis=1, tiled=True), preferred_element_type=jnp.float32
    )
    tensor_offset = lax.axis_index("tensor") * share_width
    summed_branch = lax.psum(branch.astype(jnp.bfloat16), "tensor").astype(jnp.float32)
    stream = inputs + summed_branch
    normed = rms_scale(stream, ffn_gain).astype(jnp.bfloat16)
    resid = lax.dynamic_slice_in_dim(stream, tensor_offset, share_width, 1).astype(jnp.bfloat16)
    return (
        resid.reshape(1, pair_dev, 2 * sample, share_width),
        normed.reshape(1, pair_dev, 2 * sample, width),
    )


MESH = pl.DeviceIdType.MESH
CH = 4
PARTS = 8
X1, Y1, Y2, S1A, S1B, S1C, XQ, XS, XM, SB, YB, XR, YR1, YR2, SR0, SR1, SR2, SR3, LN = range(19)
KINDS = 19


def plane_kernel(
    pair_ref, lens_ref, gain1_ref, cos_ref, sin_ref, freq_ref,
    cand_ref, wq_ref, wk_ref, wv_ref, wo_ref,
    stream_ref,
    grid_x, relay, lhs, w_in, w_out, q_send, q_recv, q_own, ss_own, ss_recv, own_lens, lens_all,
    mix_own, mix_recv, acc_own, sib_send, sib_recv, y_send, y_recv, x_send, stream,
    send_sem, recv_sem, load_sem, local_sem, store_sem,
):
    f = lax.axis_index("fsdp")
    t = lax.axis_index("tensor")
    y = t // 2
    c = t % 2
    x_dev = {"fsdp": 1 - f}
    t_y = (t + 2) % 4
    t_s = t + 1 - 2 * c
    t_sy = (t_s + 2) % 4
    y_dev = {"tensor": t_y}
    s_dev = {"tensor": t_s}
    even = f == y

    def remote(kind, j, src, dst, dev):
        return pltpu.make_async_remote_copy(
            src_ref=src, dst_ref=dst, send_sem=send_sem.at[kind, j],
            recv_sem=recv_sem.at[kind, j], device_id=dev, device_id_type=MESH,
        )

    loads = []

    def load(src, dst):
        copy = pltpu.make_async_copy(src, dst, load_sem.at[len(loads)])
        copy.start()
        loads.append(copy)

    mine = pl.multiple_of(f * 512, 512)
    other = pl.multiple_of((1 - f) * 512, 512)
    load(wq_ref.at[:, pl.ds(mine, 512)], w_in.at[:, 0:512])
    load(wq_ref.at[:, pl.ds(other, 512)], w_in.at[:, 512:1024])
    load(wk_ref, w_in.at[:, 1024:1152])
    load(wv_ref, w_in.at[:, 1152:1280])
    for r, row in enumerate((mine, other)):
        for b, block in enumerate((t, t_y, t_s, t_sy)):
            load(
                wo_ref.at[pl.ds(row, 512), pl.ds(pl.multiple_of(block * 512, 512), 512)],
                w_out.at[r * 512:(r + 1) * 512, b * 512:(b + 1) * 512],
            )

    barrier = pltpu.get_barrier_semaphore()
    for dev in (x_dev, y_dev, s_dev):
        pl.semaphore_signal(barrier, inc=1, device_id=dev, device_id_type=MESH)
    pl.semaphore_wait(barrier, 3)

    spread = jnp.broadcast_to(lens_ref[...].astype(jnp.float32), (8, 8))
    pick = lax.broadcasted_iota(jnp.int32, (8, 8), 0) == lax.broadcasted_iota(jnp.int32, (8, 8), 1)
    column = jnp.sum(jnp.where(pick, spread, 0.0), axis=1, keepdims=True)
    own_lens[...] = jnp.broadcast_to(column, (8, 128)).astype(jnp.int32)
    lens_copy = remote(LN, 0, own_lens, lens_all.at[pl.ds(pl.multiple_of(f * 8, 8), 8)], x_dev)
    lens_copy.start()
    lens_all[pl.ds(pl.multiple_of(f * 8, 8), 8), :] = own_lens[...]

    cols = pl.ds(pl.multiple_of(c * 1024, 1024), 1024)

    def place(g, j, at=0, count=2):
        return grid_x.at[pl.ds(g * 8 + 2 * j + at, count), :, cols]

    def own(j, at=0, count=2):
        return cand_ref.at[2 * j + at:2 * j + at + count]

    def hop(j):
        return relay.at[j:j + 1]

    def local_copy(j):
        return pltpu.make_async_copy(own(j), place(f, j), local_sem.at[j])

    def send_y(j):
        @pl.when(even)
        def _():
            remote(Y1, j, own(j), place(f, j), y_dev).start()

        @pl.when(jnp.logical_not(even))
        def _():
            remote(Y1, j, own(j, 1, 1), hop(j), y_dev).start()

    def far_x(j, at):
        return place(1 - f, j, at, 1)

    def forward_x(j):
        @pl.when(even)
        def _():
            remote(Y1, j, own(j, 1, 1), hop(j), y_dev).wait_recv()
            remote(X1, j, hop(j), place(f, j, 1, 1), x_dev).start()

    def forward_y(j):
        @pl.when(even)
        def _():
            remote(X1, j, own(j, 0, 1), far_x(j, 0), x_dev).wait_recv()
            remote(Y2, j, far_x(j, 0), far_x(j, 0), y_dev).start()
            remote(S1B, j, far_x(j, 0), far_x(j, 0), s_dev).start()
            local_copy(j).wait()

        @pl.when(jnp.logical_not(even))
        def _():
            remote(X1, j, hop(j), far_x(j, 1), x_dev).wait_recv()
            remote(Y2, j, far_x(j, 1), far_x(j, 1), y_dev).start()
            remote(S1B, j, far_x(j, 1), far_x(j, 1), s_dev).start()
            remote(Y1, j, own(j), place(f, j), y_dev).wait_recv()

        remote(S1A, j, place(f, j), place(f, j), s_dev).start()

    def finish_input(j):
        def last(at):
            remote(Y2, j, far_x(j, at), far_x(j, at), y_dev).wait_recv()
            remote(S1C, j, far_x(j, at), far_x(j, at), s_dev).start()
            remote(S1B, j, far_x(j, 1 - at), far_x(j, 1 - at), s_dev).wait_recv()
            remote(S1C, j, far_x(j, at), far_x(j, at), s_dev).wait_recv()

        @pl.when(even)
        def _():
            last(1)

        @pl.when(jnp.logical_not(even))
        def _():
            last(0)

        remote(S1A, j, place(f, j), place(f, j), s_dev).wait_recv()

    send_y(0)

    @pl.when(jnp.logical_not(even))
    def _():
        for j in range(CH):
            remote(X1, j, own(j, 0, 1), place(f, j, 0, 1), x_dev).start()

    send_y(1)
    send_y(2)

    @pl.when(even)
    def _():
        for j in range(CH):
            local_copy(j).start()

    for copy in loads[:4]:
        copy.wait()

    def finish(j):
        remote(XQ, j, q_send.at[j], q_recv.at[j], x_dev).wait_recv()
        remote(XS, j, ss_own.at[j], ss_recv.at[j], x_dev).wait_recv()
        total = (ss_own[j] + ss_recv[j])[0:1, :]
        scale = lax.rsqrt(total * (1.0 / 4096.0) + epsilon)
        column = jnp.broadcast_to(scale, (128, 256)).T
        for m in range(6):
            part = slice(m * 128, (m + 1) * 128)
            summed = q_own[4 * j:4 * j + 4, :, part].reshape(256, 128) + q_recv[
                j, :, part
            ].astype(jnp.float32)
            q_own[4 * j:4 * j + 4, :, part] = (summed * column).reshape(4, 64, 128)

    forward_x(0)
    forward_y(0)
    forward_x(1)
    for j in range(CH):
        finish_input(j)

        gain = gain1_ref[f]
        for g in range(2):
            values = grid_x[g * 8 + 2 * j:g * 8 + 2 * j + 2].reshape(128, 2048).astype(jnp.float32)
            squares = jnp.sum(values * values, axis=1, keepdims=True)
            ss_own[j, :, g * 128:(g + 1) * 128] = jnp.broadcast_to(squares, (128, 128)).T[0:8]
            lhs[g * 128:(g + 1) * 128, :] = (values * gain).astype(jnp.bfloat16)

        def project(n):
            return jnp.dot(
                lhs[...],
                w_in[:, pl.ds(pl.multiple_of(n * 256, 256), 256)],
                preferred_element_type=jnp.float32,
            )

        @pl.loop(0, 3)
        def _(n):
            result = project(n + 2)
            at = pl.ds(pl.multiple_of(n * 256, 256), 256)
            q_send[j, :, at] = result.astype(jnp.bfloat16)

        q_own[4 * j:4 * j + 4, :, 512:768] = project(4).reshape(4, 64, 256)
        remote(XQ, j, q_send.at[j], q_recv.at[j], x_dev).start()
        remote(XS, j, ss_own.at[j], ss_recv.at[j], x_dev).start()

        if j + 1 < CH:
            forward_y(j + 1)
        if j + 2 < CH:
            forward_x(j + 2)
        if j + 3 < CH:
            send_y(j + 3)

        @pl.loop(0, 2)
        def _(n):
            result = project(n)
            at = pl.ds(pl.multiple_of(n * 256, 256), 256)
            q_own[4 * j:4 * j + 4, :, at] = result.reshape(4, 64, 256)

        if j > 1:
            finish(j - 2)
    finish(CH - 2)
    finish(CH - 1)
    lens_copy.wait()

    lane = lax.broadcasted_iota(jnp.int32, (1, 128), 1)
    sign = jnp.where(lane < 64, -1.0, 1.0)
    slot_t = lax.broadcasted_iota(jnp.int32, (128, 128), 0)
    slot_u = lax.broadcasted_iota(jnp.int32, (128, 128), 1)

    def packed(cand):
        return ((cand % 8) // 2) * 4 + (cand // 8) * 2 + cand % 2

    def attention(k, half):
        row = half * 4 + k
        cand0, cand1 = pair_ref[row, 0], pair_ref[row, 1]
        at0, at1 = packed(cand0), packed(cand1)
        len0 = lens_all[pl.ds(cand0, 1), :]
        len1 = lens_all[pl.ds(cand1, 1), :]
        angle = len0.astype(jnp.float32) * freq_ref[...]
        shift_cos, shift_sin = jnp.cos(angle), jnp.sin(angle)
        cos0, sin0 = cos_ref[...], sin_ref[...]
        cosine = jnp.concatenate([cos0, cos0 * shift_cos - sin0 * shift_sin], axis=0)
        sine = jnp.concatenate([sin0, sin0 * shift_cos + cos0 * shift_sin], axis=0) * sign
        allowed = (slot_u <= slot_t) & (lane < jnp.where(lane < 64, len0, len1 + 64))

        def block(m):
            part = slice(m * 128, (m + 1) * 128)
            return jnp.concatenate([q_own[at0, :, part], q_own[at1, :, part]], axis=0)

        def turned(m):
            values = block(m)
            return (values * cosine + pltpu.roll(values, 64, axis=1) * sine).astype(jnp.bfloat16)

        keys = turned(4)
        value_rows = block(5).astype(jnp.bfloat16)
        queries = jnp.concatenate([turned(h) for h in range(4)], axis=0)
        scores = lax.dot_general(
            queries, keys, (((1,), (1,)), ((), ())), preferred_element_type=jnp.float32
        ) * HEAD ** (-0.5)
        scores = jnp.where(jnp.concatenate([allowed] * 4, axis=0), scores, -1e30)
        weights = jnp.exp(scores - jnp.max(scores, axis=1, keepdims=True))
        probs = weights * (1.0 / jnp.sum(weights, axis=1, keepdims=True))
        mixed = jnp.dot(
            probs.astype(jnp.bfloat16), value_rows, preferred_element_type=jnp.float32
        ).astype(jnp.bfloat16)
        for h in range(4):
            for s in range(2):
                mix_own[2 * k + s, half * 64:(half + 1) * 64, h * 128:(h + 1) * 128] = mixed[
                    h * 128 + s * 64:h * 128 + (s + 1) * 64
                ]

    def stream_at(block, k):
        return stream.at[block, k]

    def own_block(k):
        return stream_at(f * 4 + t, k)

    def far_block(k):
        return stream_at((1 - f) * 4 + t, k)

    def share(kind, ref, k, dev):
        return remote(kind, k, ref, ref, dev)

    def mix_copy(k):
        return remote(XM, k, mix_own.at[k], mix_recv.at[k], x_dev)

    def partial_copy(k):
        return remote(SB, k, sib_send.at[k], sib_recv.at[k], s_dev)

    def pair_copy(k):
        return remote(YB, k, y_send.at[k], y_recv.at[k], y_dev)

    def cross_copy(k):
        return remote(XR, k, x_send.at[k], own_block(k), x_dev)

    def project_out(k):
        mix_copy(k).wait_recv()

        def term(n):
            at = pl.ds(pl.multiple_of(n * 256, 256), 256)
            return jnp.dot(
                mix_own[k], w_out[0:512, at], preferred_element_type=jnp.float32
            ) + jnp.dot(mix_recv[k], w_out[512:1024, at], preferred_element_type=jnp.float32)

        @pl.loop(0, 4)
        def _(n):
            at = pl.ds(pl.multiple_of(n * 256, 256), 256)
            sib_send[k, :, at] = term(n + 4).astype(jnp.bfloat16)

        partial_copy(k).start()

        @pl.loop(0, 4)
        def _(n):
            acc_own[k, :, pl.ds(pl.multiple_of(n * 256, 256), 256)] = term(n)

    def add_sibling(k):
        partial_copy(k).wait_recv()
        y_send[k] = (acc_own[k, :, 512:] + sib_recv[k, :, 512:].astype(jnp.float32)).astype(
            jnp.bfloat16
        )
        pair_copy(k).start()
        acc_own[k, :, 0:512] = acc_own[k, :, 0:512] + sib_recv[k, :, 0:512].astype(jnp.float32)

    def add_rows(k):
        pair_copy(k).wait_recv()
        at = pl.ds(pl.multiple_of(t * 512, 512), 512)
        parts = []
        for half in range(2):
            rows = grid_x[pair_ref[half * 4 + k // 2, k % 2], :, at]
            part = slice(half * 64, (half + 1) * 64)
            branch = acc_own[k, part, 0:512] + y_recv[k, part, :].astype(jnp.float32)
            parts.append(rows.astype(jnp.float32) + branch)
        first = f == 0
        x_send[k] = jnp.where(first, parts[1], parts[0]).astype(jnp.bfloat16)
        cross_copy(k).start()
        stream[f * 4 + t, k] = jnp.where(first, parts[0], parts[1]).astype(jnp.bfloat16)
        share(YR1, own_block(k), k, y_dev).start()
        share(SR0, own_block(k), k, s_dev).start()

    def pass_far(k):
        remote(XR, k, x_send.at[k], far_block(k), x_dev).wait_recv()
        share(YR2, far_block(k), k, y_dev).start()
        share(SR1, far_block(k), k, s_dev).start()

    def pass_pair(k):
        near = stream_at(f * 4 + t_y, k)
        far = stream_at((1 - f) * 4 + t_y, k)
        share(YR1, near, k, y_dev).wait_recv()
        share(SR2, near, k, s_dev).start()
        share(YR2, far, k, y_dev).wait_recv()
        share(SR3, far, k, s_dev).start()

    def store_copy(k):
        return pltpu.make_async_copy(stream.at[:, k], stream_ref.at[:, k], store_sem.at[k])

    def store(k):
        share(SR0, stream_at(f * 4 + t_s, k), k, s_dev).wait_recv()
        share(SR1, stream_at((1 - f) * 4 + t_s, k), k, s_dev).wait_recv()
        share(SR2, stream_at(f * 4 + t_sy, k), k, s_dev).wait_recv()
        share(SR3, stream_at((1 - f) * 4 + t_sy, k), k, s_dev).wait_recv()
        store_copy(k).start()

    for copy in loads[4:]:
        copy.wait()
    def attend_rows(k):
        attention(k, 0)
        attention(k, 1)
        mix_copy(2 * k).start()
        mix_copy(2 * k + 1).start()

    order = [(2.0 * j - 2.5, attend_rows, j) for j in range(PARTS // 2)]
    for lag, stage in (
        (0.0, project_out), (0.8, add_sibling), (2.1, add_rows),
        (3.2, pass_far), (4.3, pass_pair), (5.4, store),
    ):
        order += [(k + lag, stage, k) for k in range(PARTS)]
    for _, stage, k in sorted(order, key=lambda item: item[0]):
        stage(k)

    for j in range(CH):

        @pl.when(even)
        def _():
            remote(Y1, j, own(j), place(f, j), y_dev).wait_send()
            remote(X1, j, hop(j), place(f, j, 1, 1), x_dev).wait_send()
            remote(Y2, j, far_x(j, 0), far_x(j, 0), y_dev).wait_send()
            remote(S1B, j, far_x(j, 0), far_x(j, 0), s_dev).wait_send()
            remote(S1C, j, far_x(j, 1), far_x(j, 1), s_dev).wait_send()

        @pl.when(jnp.logical_not(even))
        def _():
            remote(Y1, j, own(j, 1, 1), hop(j), y_dev).wait_send()
            remote(X1, j, own(j, 0, 1), place(f, j, 0, 1), x_dev).wait_send()
            remote(Y2, j, far_x(j, 1), far_x(j, 1), y_dev).wait_send()
            remote(S1B, j, far_x(j, 1), far_x(j, 1), s_dev).wait_send()
            remote(S1C, j, far_x(j, 0), far_x(j, 0), s_dev).wait_send()

        remote(S1A, j, place(f, j), place(f, j), s_dev).wait_send()
        remote(XQ, j, q_send.at[j], q_recv.at[j], x_dev).wait_send()
        remote(XS, j, ss_own.at[j], ss_recv.at[j], x_dev).wait_send()
    for j in range(PARTS):
        mix_copy(j).wait_send()
        partial_copy(j).wait_send()
        pair_copy(j).wait_send()
        cross_copy(j).wait_send()
        share(YR1, own_block(j), j, y_dev).wait_send()
        share(SR0, own_block(j), j, s_dev).wait_send()
        share(YR2, far_block(j), j, y_dev).wait_send()
        share(SR1, far_block(j), j, s_dev).wait_send()
        share(SR2, stream_at(f * 4 + t_y, j), j, s_dev).wait_send()
        share(SR3, stream_at((1 - f) * 4 + t_y, j), j, s_dev).wait_send()
        store_copy(j).wait()


def norm_kernel(stream_ref, gain2_ref, resid_ref, normed_ref):
    t = lax.axis_index("tensor")
    squares = jnp.zeros((128, 512), jnp.float32)
    for b in range(8):
        values = stream_ref[b].reshape(128, 512).astype(jnp.float32)
        squares = squares + values * values
    scale = lax.rsqrt(jnp.sum(squares, axis=1, keepdims=True) * (1.0 / 4096.0) + epsilon)
    for b in range(8):
        part = slice(b * 512, (b + 1) * 512)
        normed_ref[0, :, part] = (
            stream_ref[b].reshape(128, 512).astype(jnp.float32) * scale * gain2_ref[:, part]
        ).astype(jnp.bfloat16)
    resid_ref[0, :, 0:512] = stream_ref[2 * t].reshape(128, 512)
    resid_ref[0, :, 512:1024] = stream_ref[2 * t + 1].reshape(128, 512)


def on_plane(
    candidates, cand_lengths, pairing, attn_gain, w_query, w_key, w_value, w_out, ffn_gain
):
    half = HEAD // 2
    inv_freq = np.float32(rope_base) ** (-np.arange(half, dtype=np.float32) * 2.0 / HEAD)
    freq = np.concatenate([inv_freq, inv_freq]).astype(np.float32)[None, :]
    angles = (np.arange(64, dtype=np.float32)[:, None] * freq).astype(np.float64)
    bf16, f32 = jnp.bfloat16, jnp.float32
    vmem = pl.BlockSpec(memory_space=pltpu.VMEM)
    hbm = pl.BlockSpec(memory_space=pl.ANY)
    stream = pl.pallas_call(
        plane_kernel,
        out_shape=jax.ShapeDtypeStruct((8, PARTS, 64, 512), bf16),
        in_specs=[pl.BlockSpec(memory_space=pltpu.SMEM)] + [vmem] * 5 + [hbm] * 5,
        out_specs=hbm,
        scratch_shapes=[
            pltpu.VMEM((16, 64, 2048), bf16),
            pltpu.VMEM((CH, 64, 1024), bf16),
            pltpu.VMEM((256, 2048), bf16),
            pltpu.VMEM((2048, 1280), bf16),
            pltpu.VMEM((1024, 2048), bf16),
            pltpu.VMEM((CH, 256, 768), bf16),
            pltpu.VMEM((CH, 256, 768), bf16),
            pltpu.VMEM((16, 64, 768), f32),
            pltpu.VMEM((CH, 8, 256), f32),
            pltpu.VMEM((CH, 8, 256), f32),
            pltpu.VMEM((8, 128), jnp.int32),
            pltpu.VMEM((16, 128), jnp.int32),
            pltpu.VMEM((PARTS, 128, 512), bf16),
            pltpu.VMEM((PARTS, 128, 512), bf16),
            pltpu.VMEM((PARTS, 128, 1024), f32),
            pltpu.VMEM((PARTS, 128, 1024), bf16),
            pltpu.VMEM((PARTS, 128, 1024), bf16),
            pltpu.VMEM((PARTS, 128, 512), bf16),
            pltpu.VMEM((PARTS, 128, 512), bf16),
            pltpu.VMEM((PARTS, 64, 512), bf16),
            pltpu.VMEM((8, PARTS, 64, 512), bf16),
            pltpu.SemaphoreType.DMA((KINDS, PARTS)),
            pltpu.SemaphoreType.DMA((KINDS, PARTS)),
            pltpu.SemaphoreType.DMA((12,)),
            pltpu.SemaphoreType.DMA((CH,)),
            pltpu.SemaphoreType.DMA((PARTS,)),
        ],
        compiler_params=pltpu.CompilerParams(
            collective_id=0, has_side_effects=True, vmem_limit_bytes=58 * 2**20
        ),
    )(
        pairing[0], cand_lengths, attn_gain.reshape(2, 1, 2048),
        jnp.asarray(np.cos(angles), f32), jnp.asarray(np.sin(angles), f32), jnp.asarray(freq),
        candidates[0], w_query, w_key, w_value, w_out,
    )
    resid, normed = pl.pallas_call(
        norm_kernel,
        grid=(CH,),
        out_shape=(
            jax.ShapeDtypeStruct((CH, 128, 1024), bf16),
            jax.ShapeDtypeStruct((CH, 128, 4096), bf16),
        ),
        in_specs=[
            pl.BlockSpec((8, 2, 64, 512), lambda k: (0, k, 0, 0)),
            pl.BlockSpec((1, 4096), lambda k: (0, 0)),
        ],
        out_specs=(
            pl.BlockSpec((1, 128, 1024), lambda k: (k, 0, 0)),
            pl.BlockSpec((1, 128, 4096), lambda k: (k, 0, 0)),
        ),
        compiler_params=pltpu.CompilerParams(vmem_limit_bytes=60 * 2**20),
    )(stream, ffn_gain.reshape(1, 4096))
    return resid[None], normed[None]


def solution(mesh):
    plane = mesh.shape["fsdp"] == 2 and mesh.shape["tensor"] == 4
    return jax.shard_map(
        on_plane if plane else on_device,
        mesh=mesh,
        in_specs=(
            P("dp", "fsdp", None, "tensor"),
            P("dp", "fsdp"),
            P("dp", None, None),
            P(),
            P("fsdp", "tensor"),
            P("fsdp", "tensor"),
            P("fsdp", "tensor"),
            P("tensor", "fsdp"),
            P(),
        ),
        out_specs=(P("dp", "fsdp", None, "tensor"), P("dp", "fsdp", None, None)),
        check_vma=False,
    )
```

```python
import jax
import jax.numpy as jnp
import numpy as np
from jax import lax
from jax.experimental import pallas as pl
from jax.experimental.pallas import tpu as pltpu
from jax.sharding import PartitionSpec as P

HEAD = 128


epsilon = 1e-05
rope_base = 500000.0


def rms_scale(values, gain):
    mean_square = jnp.mean(values * values, axis=-1, keepdims=True)
    return values * lax.rsqrt(mean_square + epsilon) * gain


def positions_of(lengths, sample):
    slot_steps = jnp.arange(2 * sample, dtype=jnp.int32)
    return jnp.where(slot_steps < sample, slot_steps, lengths[..., :1] + slot_steps - sample)


def key_mask(lengths, sample):
    slot_steps = jnp.arange(2 * sample, dtype=jnp.int32)
    local_step = jnp.where(slot_steps < sample, slot_steps, slot_steps - sample)
    limit = jnp.where(slot_steps < sample, lengths[..., :1], lengths[..., 1:])
    valid = local_step < limit
    causal = slot_steps[None, :] <= slot_steps[:, None]
    return causal[None] & valid[:, None, :]


def rotate(values, positions, head_size):
    half = head_size // 2
    inv_freq = rope_base ** (-jnp.arange(half, dtype=jnp.float32) * 2.0 / head_size)
    angles = positions.astype(jnp.float32)[..., None] * inv_freq
    cosine = jnp.cos(angles)[..., None, :]
    sine_table = jnp.sin(angles)[..., None, :]
    lower = values[..., :half]
    upper = values[..., half:]
    return jnp.concatenate(
        [lower * cosine - upper * sine_table, upper * cosine + lower * sine_table], axis=-1
    )


def attend(query, key_rows, value_rows, allowed):
    pair_rows, row_count, kv_count, group_size, head_size = query.shape
    scores = jnp.einsum(
        "bqkgd,bskd->bkgqs", query, key_rows, preferred_element_type=jnp.float32
    ) * head_size ** (-0.5)
    scores = jnp.where(allowed[:, None, None], scores, -1e30)
    row_peak = jnp.max(scores, axis=-1, keepdims=True)
    weights = jnp.exp(scores - row_peak)
    prob_rows = (weights / jnp.sum(weights, axis=-1, keepdims=True)).astype(jnp.bfloat16)
    mixed_rows = jnp.einsum(
        "bkgqs,bskd->bqkgd", prob_rows, value_rows, preferred_element_type=jnp.float32
    )
    return mixed_rows.astype(jnp.bfloat16).reshape(
        pair_rows * row_count, kv_count * group_size * head_size
    )


def on_device(
    candidates, cand_lengths, pairing, attn_gain, w_query, w_key, w_value, w_out, ffn_gain
):
    fsdp_count = lax.axis_size("fsdp")
    my_index = lax.axis_index("fsdp")
    cand_dev = candidates.shape[1]
    sample = candidates.shape[2]
    share_width = candidates.shape[3]
    pair_dev = cand_dev // 2
    most_slots = max(1, cand_dev // fsdp_count)
    flat_slots = pairing[0].reshape(-1)
    slot_count = flat_slots.shape[0]
    every_slot = jnp.arange(slot_count, dtype=jnp.int32)
    matches = flat_slots[:, None] == every_slot[None, :]
    target_slot = jnp.sum(jnp.where(matches, every_slot[:, None], 0), axis=0)
    target_dev = target_slot // cand_dev
    source_dev = every_slot // cand_dev
    earlier = (
        (source_dev[:, None] == source_dev[None, :])
        & (target_dev[:, None] == target_dev[None, :])
        & (every_slot[None, :] < every_slot[:, None])
    )
    send_rank = jnp.sum(earlier.astype(jnp.int32), axis=1)
    place = target_dev * most_slots + send_rank
    arrive = source_dev * most_slots + send_rank
    own_cands = my_index * cand_dev + jnp.arange(cand_dev, dtype=jnp.int32)
    own_pick = own_cands[:, None] == every_slot[None, :]
    own_place = jnp.sum(jnp.where(own_pick, place[None, :], 0), axis=1)
    buffer_slots = jnp.arange(fsdp_count * most_slots, dtype=jnp.int32)
    sender = buffer_slots[:, None] == own_place[None, :]
    outgoing = jnp.einsum(
        "bc,csf->bsf",
        sender.astype(jnp.bfloat16),
        candidates[0],
        preferred_element_type=jnp.float32,
    ).astype(jnp.bfloat16)
    out_lengths = jnp.sum(jnp.where(sender, cand_lengths[0][None, :], 0), axis=1)
    incoming, in_lengths = (
        lax.all_to_all(
            outgoing.reshape(fsdp_count, most_slots, sample, share_width),
            "fsdp",
            split_axis=0,
            concat_axis=0,
            tiled=True,
        ),
        lax.all_to_all(
            out_lengths.reshape(fsdp_count, most_slots),
            "fsdp",
            split_axis=0,
            concat_axis=0,
            tiled=True,
        ),
    )
    slot_pick = own_cands[:, None] == every_slot[None, :]
    wanted = jnp.sum(jnp.where(slot_pick, flat_slots[None, :], 0), axis=1)
    wanted_pick = wanted[:, None] == every_slot[None, :]
    wanted_from = jnp.sum(jnp.where(wanted_pick, arrive[None, :], 0), axis=1)
    receiver = wanted_from[:, None] == buffer_slots[None, :]
    local_rows = jnp.einsum(
        "cb,bsf->csf",
        receiver.astype(jnp.bfloat16),
        incoming.reshape(-1, sample, share_width),
        preferred_element_type=jnp.float32,
    ).astype(jnp.bfloat16)
    row_lengths = (
        jnp.sum(jnp.where(receiver, in_lengths.reshape(-1)[None, :], 0), axis=1)
        .astype(jnp.int32)
        .reshape(pair_dev, 2)
    )
    full_rows = lax.all_gather(local_rows, "tensor", axis=2, tiled=True)
    width = full_rows.shape[2]
    tok_count = cand_dev * sample
    inputs = full_rows.reshape(tok_count, width).astype(jnp.float32)
    normal_rows = rms_scale(inputs, attn_gain).astype(jnp.bfloat16)
    query_cols = w_query.shape[1]
    key_cols = w_key.shape[1]
    query = jnp.dot(
        normal_rows,
        lax.all_gather(w_query, "fsdp", axis=0, tiled=True),
        preferred_element_type=jnp.float32,
    )
    key_rows = jnp.dot(
        normal_rows,
        lax.all_gather(w_key, "fsdp", axis=0, tiled=True),
        preferred_element_type=jnp.float32,
    )
    value_rows = jnp.dot(
        normal_rows,
        lax.all_gather(w_value, "fsdp", axis=0, tiled=True),
        preferred_element_type=jnp.float32,
    )
    heads_here = query_cols // HEAD
    kv_here = key_cols // HEAD
    positions = positions_of(row_lengths, sample)
    query = rotate(query.reshape(pair_dev, 2 * sample, heads_here, HEAD), positions, HEAD).astype(
        jnp.bfloat16
    )
    key_rows = rotate(
        key_rows.reshape(pair_dev, 2 * sample, kv_here, HEAD), positions, HEAD
    ).astype(jnp.bfloat16)
    value_rows = value_rows.astype(jnp.bfloat16).reshape(pair_dev, 2 * sample, kv_here, HEAD)
    query = query.reshape(pair_dev, 2 * sample, kv_here, heads_here // kv_here, HEAD)
    mixed = attend(query, key_rows, value_rows, key_mask(row_lengths, sample))
    branch = jnp.dot(
        mixed, lax.all_gather(w_out, "fsdp", axis=1, tiled=True), preferred_element_type=jnp.float32
    )
    tensor_offset = lax.axis_index("tensor") * share_width
    summed_branch = lax.psum(branch.astype(jnp.bfloat16), "tensor").astype(jnp.float32)
    stream = inputs + summed_branch
    normed = rms_scale(stream, ffn_gain).astype(jnp.bfloat16)
    resid = lax.dynamic_slice_in_dim(stream, tensor_offset, share_width, 1).astype(jnp.bfloat16)
    return (
        resid.reshape(1, pair_dev, 2 * sample, share_width),
        normed.reshape(1, pair_dev, 2 * sample, width),
    )


MESH = pl.DeviceIdType.MESH
CH = 4
PARTS = 8
X1, Y1, Y2, S1A, S1B, S1C, XQ, XS, XM, SB, YB, XR, YR1, YR2, SR0, SR1, SR2, SR3, LN = range(19)
KINDS = 19


def plane_kernel(
    pair_ref, lens_ref, gain1_ref, cos_ref, sin_ref, freq_ref,
    cand_ref, wq_ref, wk_ref, wv_ref, wo_ref,
    stream_ref,
    grid_x, relay, lhs, w_in, w_out, q_send, q_recv, q_own, ss_own, ss_recv, own_lens, lens_all,
    mix_own, mix_recv, acc_own, sib_send, sib_recv, y_send, y_recv, x_send, stream,
    send_sem, recv_sem, load_sem, local_sem, store_sem,
):
    f = lax.axis_index("fsdp")
    t = lax.axis_index("tensor")
    y = t // 2
    c = t % 2
    x_dev = {"fsdp": 1 - f}
    t_y = (t + 2) % 4
    t_s = t + 1 - 2 * c
    t_sy = (t_s + 2) % 4
    y_dev = {"tensor": t_y}
    s_dev = {"tensor": t_s}
    even = f == y

    def remote(kind, j, src, dst, dev):
        return pltpu.make_async_remote_copy(
            src_ref=src, dst_ref=dst, send_sem=send_sem.at[kind, j],
            recv_sem=recv_sem.at[kind, j], device_id=dev, device_id_type=MESH,
        )

    loads = []

    def load(src, dst):
        copy = pltpu.make_async_copy(src, dst, load_sem.at[len(loads)])
        copy.start()
        loads.append(copy)

    mine = pl.multiple_of(f * 512, 512)
    other = pl.multiple_of((1 - f) * 512, 512)
    load(wq_ref.at[:, pl.ds(mine, 512)], w_in.at[:, 0:512])
    load(wq_ref.at[:, pl.ds(other, 512)], w_in.at[:, 512:1024])
    load(wk_ref, w_in.at[:, 1024:1152])
    load(wv_ref, w_in.at[:, 1152:1280])
    for r, row in enumerate((mine, other)):
        for b, block in enumerate((t, t_y, t_s, t_sy)):
            load(
                wo_ref.at[pl.ds(row, 512), pl.ds(pl.multiple_of(block * 512, 512), 512)],
                w_out.at[r * 512:(r + 1) * 512, b * 512:(b + 1) * 512],
            )

    barrier = pltpu.get_barrier_semaphore()
    for dev in (x_dev, y_dev, s_dev):
        pl.semaphore_signal(barrier, inc=1, device_id=dev, device_id_type=MESH)
    pl.semaphore_wait(barrier, 3)

    spread = jnp.broadcast_to(lens_ref[...].astype(jnp.float32), (8, 8))
    pick = lax.broadcasted_iota(jnp.int32, (8, 8), 0) == lax.broadcasted_iota(jnp.int32, (8, 8), 1)
    column = jnp.sum(jnp.where(pick, spread, 0.0), axis=1, keepdims=True)
    own_lens[...] = jnp.broadcast_to(column, (8, 128)).astype(jnp.int32)
    lens_copy = remote(LN, 0, own_lens, lens_all.at[pl.ds(pl.multiple_of(f * 8, 8), 8)], x_dev)
    lens_copy.start()
    lens_all[pl.ds(pl.multiple_of(f * 8, 8), 8), :] = own_lens[...]

    cols = pl.ds(pl.multiple_of(c * 1024, 1024), 1024)

    def place(g, j, at=0, count=2):
        return grid_x.at[pl.ds(g * 8 + 2 * j + at, count), :, cols]

    def own(j, at=0, count=2):
        return cand_ref.at[2 * j + at:2 * j + at + count]

    def hop(j):
        return relay.at[j:j + 1]

    def local_copy(j):
        return pltpu.make_async_copy(own(j), place(f, j), local_sem.at[j])

    def send_y(j):
        @pl.when(even)
        def _():
            remote(Y1, j, own(j), place(f, j), y_dev).start()

        @pl.when(jnp.logical_not(even))
        def _():
            remote(Y1, j, own(j, 1, 1), hop(j), y_dev).start()

    def far_x(j, at):
        return place(1 - f, j, at, 1)

    def forward_x(j):
        @pl.when(even)
        def _():
            remote(Y1, j, own(j, 1, 1), hop(j), y_dev).wait_recv()
            remote(X1, j, hop(j), place(f, j, 1, 1), x_dev).start()

    def forward_y(j):
        @pl.when(even)
        def _():
            remote(X1, j, own(j, 0, 1), far_x(j, 0), x_dev).wait_recv()
            remote(Y2, j, far_x(j, 0), far_x(j, 0), y_dev).start()
            remote(S1B, j, far_x(j, 0), far_x(j, 0), s_dev).start()
            local_copy(j).wait()

        @pl.when(jnp.logical_not(even))
        def _():
            remote(X1, j, hop(j), far_x(j, 1), x_dev).wait_recv()
            remote(Y2, j, far_x(j, 1), far_x(j, 1), y_dev).start()
            remote(S1B, j, far_x(j, 1), far_x(j, 1), s_dev).start()
            remote(Y1, j, own(j), place(f, j), y_dev).wait_recv()

        remote(S1A, j, place(f, j), place(f, j), s_dev).start()

    def finish_input(j):
        def last(at):
            remote(Y2, j, far_x(j, at), far_x(j, at), y_dev).wait_recv()
            remote(S1C, j, far_x(j, at), far_x(j, at), s_dev).start()
            remote(S1B, j, far_x(j, 1 - at), far_x(j, 1 - at), s_dev).wait_recv()
            remote(S1C, j, far_x(j, at), far_x(j, at), s_dev).wait_recv()

        @pl.when(even)
        def _():
            last(1)

        @pl.when(jnp.logical_not(even))
        def _():
            last(0)

        remote(S1A, j, place(f, j), place(f, j), s_dev).wait_recv()

    send_y(0)

    @pl.when(jnp.logical_not(even))
    def _():
        for j in range(CH):
            remote(X1, j, own(j, 0, 1), place(f, j, 0, 1), x_dev).start()

    @pl.when(even)
    def _():
        for j in range(CH):
            local_copy(j).start()

    for copy in loads[:4]:
        copy.wait()

    def finish(j):
        remote(XQ, j, q_send.at[j], q_recv.at[j], x_dev).wait_recv()
        remote(XS, j, ss_own.at[j], ss_recv.at[j], x_dev).wait_recv()
        total = (ss_own[j] + ss_recv[j])[0:1, :]
        scale = lax.rsqrt(total * (1.0 / 4096.0) + epsilon)
        column = jnp.broadcast_to(scale, (128, 256)).T
        for m in range(6):
            part = slice(m * 128, (m + 1) * 128)
            summed = q_own[4 * j:4 * j + 4, :, part].reshape(256, 128) + q_recv[
                j, :, part
            ].astype(jnp.float32)
            q_own[4 * j:4 * j + 4, :, part] = (summed * column).reshape(4, 64, 128)

    forward_x(0)
    send_y(1)
    for j in range(CH):
        forward_y(j)
        if j + 1 < CH:
            forward_x(j + 1)
        if j + 2 < CH:
            send_y(j + 2)
        finish_input(j)

        gain = gain1_ref[f]
        for g in range(2):
            values = grid_x[g * 8 + 2 * j:g * 8 + 2 * j + 2].reshape(128, 2048).astype(jnp.float32)
            squares = jnp.sum(values * values, axis=1, keepdims=True)
            ss_own[j, :, g * 128:(g + 1) * 128] = jnp.broadcast_to(squares, (128, 128)).T[0:8]
            lhs[g * 128:(g + 1) * 128, :] = (values * gain).astype(jnp.bfloat16)

        def project(n):
            return jnp.dot(
                lhs[...],
                w_in[:, pl.ds(pl.multiple_of(n * 256, 256), 256)],
                preferred_element_type=jnp.float32,
            )

        @pl.loop(0, 3)
        def _(n):
            result = project(n + 2)
            at = pl.ds(pl.multiple_of(n * 256, 256), 256)
            q_send[j, :, at] = result.astype(jnp.bfloat16)

        q_own[4 * j:4 * j + 4, :, 512:768] = project(4).reshape(4, 64, 256)
        remote(XQ, j, q_send.at[j], q_recv.at[j], x_dev).start()
        remote(XS, j, ss_own.at[j], ss_recv.at[j], x_dev).start()

        @pl.loop(0, 2)
        def _(n):
            result = project(n)
            at = pl.ds(pl.multiple_of(n * 256, 256), 256)
            q_own[4 * j:4 * j + 4, :, at] = result.reshape(4, 64, 256)

        if j > 1:
            finish(j - 2)
    finish(CH - 2)
    finish(CH - 1)
    lens_copy.wait()

    lane = lax.broadcasted_iota(jnp.int32, (1, 128), 1)
    sign = jnp.where(lane < 64, -1.0, 1.0)
    slot_t = lax.broadcasted_iota(jnp.int32, (128, 128), 0)
    slot_u = lax.broadcasted_iota(jnp.int32, (128, 128), 1)

    def packed(cand):
        return ((cand % 8) // 2) * 4 + (cand // 8) * 2 + cand % 2

    def attention(k, half):
        row = half * 4 + k
        cand0, cand1 = pair_ref[row, 0], pair_ref[row, 1]
        at0, at1 = packed(cand0), packed(cand1)
        len0 = lens_all[pl.ds(cand0, 1), :]
        len1 = lens_all[pl.ds(cand1, 1), :]
        angle = len0.astype(jnp.float32) * freq_ref[...]
        shift_cos, shift_sin = jnp.cos(angle), jnp.sin(angle)
        cos0, sin0 = cos_ref[...], sin_ref[...]
        cosine = jnp.concatenate([cos0, cos0 * shift_cos - sin0 * shift_sin], axis=0)
        sine = jnp.concatenate([sin0, sin0 * shift_cos + cos0 * shift_sin], axis=0) * sign
        allowed = (slot_u <= slot_t) & (lane < jnp.where(lane < 64, len0, len1 + 64))

        def block(m):
            part = slice(m * 128, (m + 1) * 128)
            return jnp.concatenate([q_own[at0, :, part], q_own[at1, :, part]], axis=0)

        def turned(m):
            values = block(m)
            return (values * cosine + pltpu.roll(values, 64, axis=1) * sine).astype(jnp.bfloat16)

        keys = turned(4)
        value_rows = block(5).astype(jnp.bfloat16)
        queries = jnp.concatenate([turned(h) for h in range(4)], axis=0)
        scores = lax.dot_general(
            queries, keys, (((1,), (1,)), ((), ())), preferred_element_type=jnp.float32
        ) * HEAD ** (-0.5)
        scores = jnp.where(jnp.concatenate([allowed] * 4, axis=0), scores, -1e30)
        weights = jnp.exp(scores - jnp.max(scores, axis=1, keepdims=True))
        probs = weights * (1.0 / jnp.sum(weights, axis=1, keepdims=True))
        mixed = jnp.dot(
            probs.astype(jnp.bfloat16), value_rows, preferred_element_type=jnp.float32
        ).astype(jnp.bfloat16)
        for h in range(4):
            for s in range(2):
                mix_own[2 * k + s, half * 64:(half + 1) * 64, h * 128:(h + 1) * 128] = mixed[
                    h * 128 + s * 64:h * 128 + (s + 1) * 64
                ]

    def stream_at(block, k):
        return stream.at[block, k]

    def own_block(k):
        return stream_at(f * 4 + t, k)

    def far_block(k):
        return stream_at((1 - f) * 4 + t, k)

    def share(kind, ref, k, dev):
        return remote(kind, k, ref, ref, dev)

    def mix_copy(k):
        return remote(XM, k, mix_own.at[k], mix_recv.at[k], x_dev)

    def partial_copy(k):
        return remote(SB, k, sib_send.at[k], sib_recv.at[k], s_dev)

    def pair_copy(k):
        return remote(YB, k, y_send.at[k], y_recv.at[k], y_dev)

    def cross_copy(k):
        return remote(XR, k, x_send.at[k], own_block(k), x_dev)

    def project_out(k):
        mix_copy(k).wait_recv()

        def term(n):
            at = pl.ds(pl.multiple_of(n * 256, 256), 256)
            return jnp.dot(
                mix_own[k], w_out[0:512, at], preferred_element_type=jnp.float32
            ) + jnp.dot(mix_recv[k], w_out[512:1024, at], preferred_element_type=jnp.float32)

        @pl.loop(0, 4)
        def _(n):
            at = pl.ds(pl.multiple_of(n * 256, 256), 256)
            sib_send[k, :, at] = term(n + 4).astype(jnp.bfloat16)

        partial_copy(k).start()

        @pl.loop(0, 4)
        def _(n):
            acc_own[k, :, pl.ds(pl.multiple_of(n * 256, 256), 256)] = term(n)

    def add_sibling(k):
        partial_copy(k).wait_recv()
        y_send[k] = (acc_own[k, :, 512:] + sib_recv[k, :, 512:].astype(jnp.float32)).astype(
            jnp.bfloat16
        )
        pair_copy(k).start()
        acc_own[k, :, 0:512] = acc_own[k, :, 0:512] + sib_recv[k, :, 0:512].astype(jnp.float32)

    def add_rows(k):
        pair_copy(k).wait_recv()
        at = pl.ds(pl.multiple_of(t * 512, 512), 512)
        parts = []
        for half in range(2):
            rows = grid_x[pair_ref[half * 4 + k // 2, k % 2], :, at]
            part = slice(half * 64, (half + 1) * 64)
            branch = acc_own[k, part, 0:512] + y_recv[k, part, :].astype(jnp.float32)
            parts.append(rows.astype(jnp.float32) + branch)
        first = f == 0
        x_send[k] = jnp.where(first, parts[1], parts[0]).astype(jnp.bfloat16)
        cross_copy(k).start()
        stream[f * 4 + t, k] = jnp.where(first, parts[0], parts[1]).astype(jnp.bfloat16)
        share(YR1, own_block(k), k, y_dev).start()
        share(SR0, own_block(k), k, s_dev).start()

    def pass_far(k):
        remote(XR, k, x_send.at[k], far_block(k), x_dev).wait_recv()
        share(YR2, far_block(k), k, y_dev).start()
        share(SR1, far_block(k), k, s_dev).start()

    def pass_pair(k):
        near = stream_at(f * 4 + t_y, k)
        far = stream_at((1 - f) * 4 + t_y, k)
        share(YR1, near, k, y_dev).wait_recv()
        share(SR2, near, k, s_dev).start()
        share(YR2, far, k, y_dev).wait_recv()
        share(SR3, far, k, s_dev).start()

    def store_copy(k):
        return pltpu.make_async_copy(stream.at[:, k], stream_ref.at[:, k], store_sem.at[k])

    def store(k):
        share(SR0, stream_at(f * 4 + t_s, k), k, s_dev).wait_recv()
        share(SR1, stream_at((1 - f) * 4 + t_s, k), k, s_dev).wait_recv()
        share(SR2, stream_at(f * 4 + t_sy, k), k, s_dev).wait_recv()
        share(SR3, stream_at((1 - f) * 4 + t_sy, k), k, s_dev).wait_recv()
        store_copy(k).start()

    for copy in loads[4:]:
        copy.wait()
    def attend_rows(k):
        attention(k, 0)
        attention(k, 1)
        mix_copy(2 * k).start()
        mix_copy(2 * k + 1).start()

    order = [(2.0 * j - 2.5, attend_rows, j) for j in range(PARTS // 2)]
    for lag, stage in (
        (0.0, project_out), (0.8, add_sibling), (2.1, add_rows),
        (3.2, pass_far), (4.3, pass_pair), (5.4, store),
    ):
        order += [(k + lag, stage, k) for k in range(PARTS)]
    for _, stage, k in sorted(order, key=lambda item: item[0]):
        stage(k)

    for j in range(CH):

        @pl.when(even)
        def _():
            remote(Y1, j, own(j), place(f, j), y_dev).wait_send()
            remote(X1, j, hop(j), place(f, j, 1, 1), x_dev).wait_send()
            remote(Y2, j, far_x(j, 0), far_x(j, 0), y_dev).wait_send()
            remote(S1B, j, far_x(j, 0), far_x(j, 0), s_dev).wait_send()
            remote(S1C, j, far_x(j, 1), far_x(j, 1), s_dev).wait_send()

        @pl.when(jnp.logical_not(even))
        def _():
            remote(Y1, j, own(j, 1, 1), hop(j), y_dev).wait_send()
            remote(X1, j, own(j, 0, 1), place(f, j, 0, 1), x_dev).wait_send()
            remote(Y2, j, far_x(j, 1), far_x(j, 1), y_dev).wait_send()
            remote(S1B, j, far_x(j, 1), far_x(j, 1), s_dev).wait_send()
            remote(S1C, j, far_x(j, 0), far_x(j, 0), s_dev).wait_send()

        remote(S1A, j, place(f, j), place(f, j), s_dev).wait_send()
        remote(XQ, j, q_send.at[j], q_recv.at[j], x_dev).wait_send()
        remote(XS, j, ss_own.at[j], ss_recv.at[j], x_dev).wait_send()
    for j in range(PARTS):
        mix_copy(j).wait_send()
        partial_copy(j).wait_send()
        pair_copy(j).wait_send()
        cross_copy(j).wait_send()
        share(YR1, own_block(j), j, y_dev).wait_send()
        share(SR0, own_block(j), j, s_dev).wait_send()
        share(YR2, far_block(j), j, y_dev).wait_send()
        share(SR1, far_block(j), j, s_dev).wait_send()
        share(SR2, stream_at(f * 4 + t_y, j), j, s_dev).wait_send()
        share(SR3, stream_at((1 - f) * 4 + t_y, j), j, s_dev).wait_send()
        store_copy(j).wait()


def norm_kernel(stream_ref, gain2_ref, resid_ref, normed_ref):
    t = lax.axis_index("tensor")
    squares = jnp.zeros((128, 512), jnp.float32)
    for b in range(8):
        values = stream_ref[b].reshape(128, 512).astype(jnp.float32)
        squares = squares + values * values
    scale = lax.rsqrt(jnp.sum(squares, axis=1, keepdims=True) * (1.0 / 4096.0) + epsilon)
    for b in range(8):
        part = slice(b * 512, (b + 1) * 512)
        normed_ref[0, :, part] = (
            stream_ref[b].reshape(128, 512).astype(jnp.float32) * scale * gain2_ref[:, part]
        ).astype(jnp.bfloat16)
    resid_ref[0, :, 0:512] = stream_ref[2 * t].reshape(128, 512)
    resid_ref[0, :, 512:1024] = stream_ref[2 * t + 1].reshape(128, 512)


def on_plane(
    candidates, cand_lengths, pairing, attn_gain, w_query, w_key, w_value, w_out, ffn_gain
):
    half = HEAD // 2
    inv_freq = np.float32(rope_base) ** (-np.arange(half, dtype=np.float32) * 2.0 / HEAD)
    freq = np.concatenate([inv_freq, inv_freq]).astype(np.float32)[None, :]
    angles = (np.arange(64, dtype=np.float32)[:, None] * freq).astype(np.float64)
    bf16, f32 = jnp.bfloat16, jnp.float32
    vmem = pl.BlockSpec(memory_space=pltpu.VMEM)
    hbm = pl.BlockSpec(memory_space=pl.ANY)
    stream = pl.pallas_call(
        plane_kernel,
        out_shape=jax.ShapeDtypeStruct((8, PARTS, 64, 512), bf16),
        in_specs=[pl.BlockSpec(memory_space=pltpu.SMEM)] + [vmem] * 5 + [hbm] * 5,
        out_specs=hbm,
        scratch_shapes=[
            pltpu.VMEM((16, 64, 2048), bf16),
            pltpu.VMEM((CH, 64, 1024), bf16),
            pltpu.VMEM((256, 2048), bf16),
            pltpu.VMEM((2048, 1280), bf16),
            pltpu.VMEM((1024, 2048), bf16),
            pltpu.VMEM((CH, 256, 768), bf16),
            pltpu.VMEM((CH, 256, 768), bf16),
            pltpu.VMEM((16, 64, 768), f32),
            pltpu.VMEM((CH, 8, 256), f32),
            pltpu.VMEM((CH, 8, 256), f32),
            pltpu.VMEM((8, 128), jnp.int32),
            pltpu.VMEM((16, 128), jnp.int32),
            pltpu.VMEM((PARTS, 128, 512), bf16),
            pltpu.VMEM((PARTS, 128, 512), bf16),
            pltpu.VMEM((PARTS, 128, 1024), f32),
            pltpu.VMEM((PARTS, 128, 1024), bf16),
            pltpu.VMEM((PARTS, 128, 1024), bf16),
            pltpu.VMEM((PARTS, 128, 512), bf16),
            pltpu.VMEM((PARTS, 128, 512), bf16),
            pltpu.VMEM((PARTS, 64, 512), bf16),
            pltpu.VMEM((8, PARTS, 64, 512), bf16),
            pltpu.SemaphoreType.DMA((KINDS, PARTS)),
            pltpu.SemaphoreType.DMA((KINDS, PARTS)),
            pltpu.SemaphoreType.DMA((12,)),
            pltpu.SemaphoreType.DMA((CH,)),
            pltpu.SemaphoreType.DMA((PARTS,)),
        ],
        compiler_params=pltpu.CompilerParams(
            collective_id=0, has_side_effects=True, vmem_limit_bytes=58 * 2**20
        ),
    )(
        pairing[0], cand_lengths, attn_gain.reshape(2, 1, 2048),
        jnp.asarray(np.cos(angles), f32), jnp.asarray(np.sin(angles), f32), jnp.asarray(freq),
        candidates[0], w_query, w_key, w_value, w_out,
    )
    resid, normed = pl.pallas_call(
        norm_kernel,
        grid=(CH,),
        out_shape=(
            jax.ShapeDtypeStruct((CH, 128, 1024), bf16),
            jax.ShapeDtypeStruct((CH, 128, 4096), bf16),
        ),
        in_specs=[
            pl.BlockSpec((8, 2, 64, 512), lambda k: (0, k, 0, 0)),
            pl.BlockSpec((1, 4096), lambda k: (0, 0)),
        ],
        out_specs=(
            pl.BlockSpec((1, 128, 1024), lambda k: (k, 0, 0)),
            pl.BlockSpec((1, 128, 4096), lambda k: (k, 0, 0)),
        ),
        compiler_params=pltpu.CompilerParams(vmem_limit_bytes=60 * 2**20),
    )(stream, ffn_gain.reshape(1, 4096))
    return resid[None], normed[None]


def solution(mesh):
    plane = mesh.shape["fsdp"] == 2 and mesh.shape["tensor"] == 4
    return jax.shard_map(
        on_plane if plane else on_device,
        mesh=mesh,
        in_specs=(
            P("dp", "fsdp", None, "tensor"),
            P("dp", "fsdp"),
            P("dp", None, None),
            P(),
            P("fsdp", "tensor"),
            P("fsdp", "tensor"),
            P("fsdp", "tensor"),
            P("tensor", "fsdp"),
            P(),
        ),
        out_specs=(P("dp", "fsdp", None, "tensor"), P("dp", "fsdp", None, None)),
        check_vma=False,
    )
```
